512 devices in a mesh: section: 32 (over y_lo, x, core), head: 16 (over y_hi, z).
Axes of the slice: x: 4, y: 8 (y_hi: 2, y_lo: 4; y = y_hi * 4 + y_lo), z: 8, core: 2. Of those that a mesh axis runs over, the one named last changes fastest.
Arguments:
- tokens: bfloat16 [16384, 2048], P('section', 'head'), may hold values from -6 to 6
- norm_gain: float32 [2048], replicated, may hold values from 0.1 to 1.9
- x_weight: bfloat16 [2048, 4096], P(None, 'head'), may hold values from -0.125 to 0.125
- gate_weight: bfloat16 [2048, 4096], P(None, 'head'), may hold values from -0.125 to 0.125
- dt_weight: bfloat16 [2048, 64], P(None, 'head'), may hold values from -0.125 to 0.125
- dt_bias: float32 [64], P('head'), may hold values from -3 to 1
- decay_rate: float32 [64], P('head'), may hold values from 1e-05 to 0.5
- skip_gain: float32 [64], P('head'), may hold values from 0.5 to 1.5
- bc_weight: bfloat16 [2048, 256], P('head'), may hold values from -0.125 to 0.125
- out_gain: float32 [4096], P('head'), may hold values from 0.1 to 1.9
- out_weight: bfloat16 [4096, 2048], P('head'), may hold values from -0.09375 to 0.09375
Outputs:
- mixed: float32 [16384, 2048], P('section', 'head')
The draws below stay inside these ranges and needn't reach their ends.
All inputs are finite; a program needn't handle non-finite values.
Results may differ from the reference program's by a relative error of at most 0.0053.
Values may be sent and summed in bfloat16 or wider, within the bound.
No kernel may reach another device: no remote copies, remote signals or barrier semaphores. Data moves between devices by JAX's collectives and lax.ppermute only.
A program may use at most 64 MiB of HBM per device.

```python
import math
import jax
import jax.numpy as jnp
from jax import lax

D = 2048
HEADS = 64
STATE = 128
BLOCK = 256
INNER = 4096
SEQ = 16384


def steps_of(own_key, dims, shards, low, largest):
    level = 1.0
    for position, blocks in shards:
        steps = jax.random.uniform(jax.random.fold_in(jax.random.fold_in(own_key, 6), position), (blocks,), jnp.float32, low / len(shards), largest / len(shards))
        level = level * jnp.repeat(jnp.exp(steps), dims[position] // blocks).reshape((-1,) + (1,) * (len(dims) - 1 - position))
    return level


def bell_draw(own_key, shape, width, limit, split=(), kind=jnp.bfloat16):
    values = jax.random.normal(own_key, shape, jnp.float32) * width
    if len(split) > 0:
        values = steps_of(own_key, shape, split, -0.22, 0.18) * values
    return jnp.clip(values, min=-limit, max=limit).astype(kind)


def setup_inputs(seed: int = 0) -> dict:
    streams_of = jax.random.split(jax.random.key(seed), 12)
    return {
        "tokens": bell_draw(streams_of[0], (SEQ, D), 1.0, 6.0, ((0, 32), (1, 16))),
        "norm_gain": jnp.clip(1.0 + 0.18 * jax.random.normal(streams_of[1], (D,), jnp.float32), 0.1, 1.9),
        "x_weight": bell_draw(streams_of[2], (D, INNER), D ** -0.5, 0.125, ((1, 16),)),
        "gate_weight": bell_draw(streams_of[3], (D, INNER), D ** -0.5, 0.125, ((1, 16),)),
        "dt_weight": bell_draw(streams_of[4], (D, HEADS), D ** -0.5, 0.125, ((1, 16),)),
        "dt_bias": jnp.clip(-3.0 + 4.0 * jax.random.uniform(streams_of[5], (HEADS,), jnp.float32) ** steps_of(streams_of[5], (HEADS,), ((0, 16),), -0.2, 0.2), -3.0, 1.0),
        "decay_rate": jnp.clip(jnp.exp(math.log(0.5) - 10.819778 * jax.random.uniform(streams_of[6], (HEADS,), jnp.float32) ** steps_of(streams_of[6], (HEADS,), ((0, 16),), -0.2, 0.2)), 9.999999747378752e-06, 0.5),
        "skip_gain": jnp.clip(0.5 + 1.0 * jax.random.uniform(streams_of[7], (HEADS,), jnp.float32) ** steps_of(streams_of[7], (HEADS,), ((0, 16),), -0.2, 0.2), 0.5, 1.5),
        "bc_weight": bell_draw(streams_of[8], (D, 2 * STATE), D ** -0.5, 0.125, ((0, 16),)),
        "out_gain": jnp.clip(1.0 + 0.18 * jax.random.normal(streams_of[9], (INNER,), jnp.float32), 0.1, 1.9),
        "out_weight": bell_draw(streams_of[10], (INNER, D), INNER ** -0.5, 0.09375, ((0, 16),)),
    }


eps = 1e-05
highest = lax.Precision.HIGHEST

def block_pass(state, pieces):
    inputs, writes, reads, step, decay = pieces
    cums = jnp.cumsum(decay, axis=0)
    cums_t = cums.T
    diff = cums_t[:, :, None] - cums_t[:, None, :]
    count = cums.shape[0]
    lower = lax.broadcasted_iota(jnp.int32, (count, count), 0) >= lax.broadcasted_iota(jnp.int32, (count, count), 1)
    weight = jnp.exp(jnp.where(lower[None, :, :], diff, -jnp.inf))
    scores = jnp.dot(reads, writes.T, precision=highest)
    mixing = weight * scores[None, :, :] * step.T[:, None, :]
    result = jnp.einsum('hts,shp->thp', mixing, inputs, precision=highest)
    carried = jnp.einsum('tn,hpn->thp', reads, state, precision=highest)
    result = result + jnp.exp(cums)[:, :, None] * carried
    tail = jnp.exp(cums[-1][None, :] - cums) * step
    fresh = jnp.einsum('sh,shp,sn->hpn', tail, inputs, writes, precision=highest)
    new_state = jnp.exp(cums[-1])[:, None, None] * state + fresh
    return (new_state, result)

def reference(tokens, norm_gain, x_weight, gate_weight, dt_weight, dt_bias, decay_rate, skip_gain, bc_weight, out_gain, out_weight):
    length = tokens.shape[0]
    heads = decay_rate.shape[0]
    inner = x_weight.shape[1]
    size_p = inner // heads
    state_n = bc_weight.shape[1] // 2
    tok_real = tokens.astype(jnp.float32)
    scale = lax.rsqrt(lax.optimization_barrier(jnp.mean(tok_real * tok_real, axis=-1, keepdims=True)) + eps)
    normed = (tok_real * scale * norm_gain).astype(jnp.bfloat16)
    inputs = jax.nn.silu(jnp.dot(normed, x_weight, preferred_element_type=jnp.float32))
    gate = jnp.dot(normed, gate_weight, preferred_element_type=jnp.float32)
    step = jax.nn.softplus(jnp.dot(normed, dt_weight, preferred_element_type=jnp.float32) + dt_bias)
    decay = -decay_rate * step
    both = jnp.dot(normed, bc_weight, preferred_element_type=jnp.float32)
    writes = both[:, :state_n]
    reads = both[:, state_n:]
    blocks = length // BLOCK
    in3 = inputs.reshape(length, heads, size_p)
    pieces = (in3.reshape(blocks, BLOCK, heads, size_p), writes.reshape(blocks, BLOCK, state_n), reads.reshape(blocks, BLOCK, state_n), step.reshape(blocks, BLOCK, heads), decay.reshape(blocks, BLOCK, heads))
    start = jnp.zeros((heads, size_p, state_n), jnp.float32)
    final, outs = lax.scan(block_pass, start, pieces)
    result = outs.reshape(length, heads, size_p) + skip_gain[None, :, None] * in3
    gated = result * jax.nn.silu(gate.reshape(length, heads, size_p))
    gated = gated * lax.rsqrt(lax.optimization_barrier(jnp.mean(gated * gated, axis=-1, keepdims=True)) + eps)
    ynorm = (gated.reshape(length, inner) * out_gain).astype(jnp.bfloat16)
    delta = jnp.dot(ynorm, out_weight, preferred_element_type=jnp.float32)
    return tok_real + delta
```

```python
import jax
import jax.numpy as jnp
from jax import lax
from jax.sharding import PartitionSpec as P

BLOCK = 256


eps = 1e-05
highest = lax.Precision.HIGHEST


def block_pass(state, pieces):
    inputs, writes, reads, step, decay = pieces
    cums = jnp.cumsum(decay, axis=0)
    cums_t = cums.T
    diff = cums_t[:, :, None] - cums_t[:, None, :]
    count = cums.shape[0]
    lower = lax.broadcasted_iota(jnp.int32, (count, count), 0) >= lax.broadcasted_iota(
        jnp.int32, (count, count), 1
    )
    weight = jnp.exp(jnp.where(lower[None, :, :], diff, -jnp.inf))
    scores = jnp.dot(reads, writes.T, precision=highest)
    mixing = weight * scores[None, :, :] * step.T[:, None, :]
    result = jnp.einsum("hts,shp->thp", mixing, inputs, precision=highest)
    carried = jnp.einsum("tn,hpn->thp", reads, state, precision=highest)
    result = result + jnp.exp(cums)[:, :, None] * carried
    tail = jnp.exp(cums[-1][None, :] - cums) * step
    fresh = jnp.einsum("sh,shp,sn->hpn", tail, inputs, writes, precision=highest)
    new_state = jnp.exp(cums[-1])[:, None, None] * state + fresh
    return (new_state, result)


def gather_head(block):
    copies = jnp.broadcast_to(block[None], (lax.axis_size("head"),) + block.shape)
    return lax.all_to_all(copies, "head", 0, 0)


def incoming_state(local_state, log_decay):
    sections = lax.axis_size("section")
    heads, size_p, state_n = local_state.shape
    lines = heads * size_p // sections
    chunks = local_state.reshape(sections, lines, state_n)
    extra = jnp.repeat(log_decay, sections // heads)[:, None, None]
    extra = jnp.broadcast_to(extra, (sections, lines, state_n))
    sent = lax.all_to_all(jnp.concatenate([chunks, extra], 1), "section", 0, 0)
    got, logs = sent[:, :lines], sent[:, lines, 0]
    until = jnp.cumsum(logs)
    ahead = jnp.concatenate([jnp.zeros_like(until[:1]), until[:-1]])
    place = jnp.arange(sections)
    before = place[:, None] > place[None, :]
    span = jnp.where(before, ahead[:, None] - until[None, :], -jnp.inf)
    mixed = jnp.einsum("sr,rln->sln", jnp.exp(span), got, precision=highest)
    back = lax.all_to_all(mixed, "section", 0, 0)
    return back.reshape(heads, size_p, state_n)


def local(
    tokens,
    norm_gain,
    x_weight,
    gate_weight,
    dt_weight,
    dt_bias,
    decay_rate,
    skip_gain,
    bc_weight,
    out_gain,
    out_weight,
):
    rows, own_width = tokens.shape
    heads = decay_rate.shape[0]
    inner = x_weight.shape[1]
    size_p = inner // heads
    state_n = bc_weight.shape[1] // 2
    groups = lax.axis_size("head")
    tok_real = tokens.astype(jnp.float32)
    packed = jnp.concatenate([tokens, bc_weight[:, :state_n], bc_weight[:, state_n:]], 0)
    whole = gather_head(packed)
    write_weight = whole[:, rows : rows + own_width].reshape(groups * own_width, state_n)
    read_weight = whole[:, rows + own_width :].reshape(groups * own_width, state_n)
    whole_real = whole[:, :rows].transpose(1, 0, 2).reshape(rows, -1).astype(jnp.float32)
    scale = lax.rsqrt(jnp.mean(whole_real * whole_real, axis=-1, keepdims=True) + eps)
    normed = (whole_real * scale * norm_gain).astype(jnp.bfloat16)
    in_raw = jnp.dot(normed, x_weight, preferred_element_type=jnp.float32)
    gate = jnp.dot(normed, gate_weight, preferred_element_type=jnp.float32)
    step_raw = jnp.dot(normed, dt_weight, preferred_element_type=jnp.float32)
    writes = jnp.dot(normed, write_weight, preferred_element_type=jnp.float32)
    reads = jnp.dot(normed, read_weight, preferred_element_type=jnp.float32)
    inputs = jax.nn.silu(in_raw).reshape(rows, heads, size_p)
    step = jax.nn.softplus(step_raw + dt_bias)
    decay = -decay_rate * step
    blocks = rows // BLOCK
    pieces = (
        inputs.reshape(blocks, BLOCK, heads, size_p),
        writes.reshape(blocks, BLOCK, state_n),
        reads.reshape(blocks, BLOCK, state_n),
        step.reshape(blocks, BLOCK, heads),
        decay.reshape(blocks, BLOCK, heads),
    )
    zero_state = jnp.zeros((heads, size_p, state_n), jnp.float32)
    local_state, outs = lax.scan(block_pass, zero_state, pieces)
    running = jnp.cumsum(decay, axis=0)
    state_in = incoming_state(local_state, running[-1])
    carried = jnp.einsum("tn,hpn->thp", reads, state_in, precision=highest)
    result = outs.reshape(rows, heads, size_p) + jnp.exp(running)[:, :, None] * carried
    result = result + skip_gain[None, :, None] * inputs
    gated = result * jax.nn.silu(gate.reshape(rows, heads, size_p))
    gated = gated * lax.rsqrt(jnp.mean(gated * gated, axis=-1, keepdims=True) + eps)
    ynorm = (gated.reshape(rows, inner) * out_gain).astype(jnp.bfloat16)
    shares = jnp.dot(ynorm, out_weight, preferred_element_type=jnp.float32)
    shares = shares.astype(jnp.bfloat16).reshape(rows, groups, own_width).transpose(1, 0, 2)
    shares = lax.all_to_all(shares, "head", 0, 0)
    return tok_real + jnp.sum(shares.astype(jnp.float32), axis=0)


def solution(mesh):
    return jax.shard_map(
        local,
        mesh=mesh,
        in_specs=(
            P("section", "head"),
            P(),
            P(None, "head"),
            P(None, "head"),
            P(None, "head"),
            P("head"),
            P("head"),
            P("head"),
            P("head", None),
            P("head"),
            P("head", None),
        ),
        out_specs=P("section", "head"),
        check_vma=False,
    )
```

```python
import functools

import jax
import jax.numpy as jnp
from jax import lax
from jax.experimental import pallas as pl
from jax.experimental.pallas import tpu as pltpu
from jax.sharding import PartitionSpec as P

eps = 1e-05
highest = lax.Precision.HIGHEST
RING = 8
SIDE = 2
f32 = jnp.float32
bf16 = jnp.bfloat16
VMEM_BYTES = 40 * 1024 * 1024


def dot(a, b, dims=((1,), (0,)), precision=None):
    return lax.dot_general(a, b, (dims, ((), ())), precision=precision, preferred_element_type=f32)


def silu(v):
    return v / (1.0 + jnp.exp(-v))


def softplus(v):
    return jnp.maximum(v, 0.0) + jnp.log1p(jnp.exp(-jnp.abs(v)))


def iota(shape, dim):
    return lax.broadcasted_iota(jnp.int32, shape, dim)


def spread(heads_on_lanes, width, size_p):
    lanes = heads_on_lanes.shape[1]
    pick = (iota((lanes, width), 1) // size_p == iota((lanes, width), 0)).astype(f32)
    return dot(heads_on_lanes, pick, precision=highest)


def column(row, rows, size_p, first):
    lanes = row.shape[1]
    mine = iota((rows, lanes), 1) == iota((rows, lanes), 0) // size_p + first
    return jnp.sum(jnp.where(mine, row, 0.0), axis=1, keepdims=True)


def log_rows(row):
    high = row.astype(bf16).astype(f32)
    low = row - high
    return jnp.concatenate([high, low, jnp.zeros((14, row.shape[1]), f32)], 0).astype(bf16)


def log_row(ref, half):
    tail = ref[half : half + 16].astype(f32)
    return tail[0:1] + tail[1:2]


def project_kernel(heads, size_p, place, *refs):
    blocks = refs[:RING]
    (gain, x_weight, dt_weight, bc_one, bc_two, small) = refs[RING : RING + 6]
    (normed, x_out, writes_out, reads_out, cums_out, step_out, mine, theirs, state) = refs[RING + 6 :]
    rows = normed.shape[0]
    own = blocks[0].shape[1]
    side, turn, core = place[0], place[1], place[2]

    def parts():
        for k in range(RING):
            for j in range(SIDE):
                head = lax.rem(side + j, SIDE) * RING + lax.rem(turn + k, RING)
                yield blocks[k][j * rows : (j + 1) * rows, :].astype(f32), head

    squares = jnp.zeros((rows, own), f32)
    for value, _ in parts():
        squares = squares + value * value
    mean = jnp.sum(squares, axis=1, keepdims=True) / (RING * SIDE * own)
    scale = lax.rsqrt(mean + eps)
    for value, head in parts():
        spot = pl.multiple_of(head * own, own)
        normed[:, pl.ds(spot, own)] = (value * scale * gain[pl.ds(head, 1), :]).astype(bf16)
    whole = normed[...]
    step = softplus(dot(whole, dt_weight[...]) + small[0:1, :])
    decay = -small[1:2, :] * step
    lower = (iota((rows, rows), 0) >= iota((rows, rows), 1)).astype(f32)
    cums = dot(lower, decay, precision=highest)
    one = dot(whole, bc_one[...])
    two = dot(whole, bc_two[...])
    writes = jnp.where(core == 0, one, two)
    reads = jnp.where(core == 0, two, one)
    x = silu(dot(whole, x_weight[...]))
    x_out[...] = x
    writes_out[...] = writes
    reads_out[...] = reads
    cums_out[...] = cums
    step_out[...] = step
    last = cums[rows - 1 : rows, :]
    tail = spread(jnp.exp(last - cums) * step, heads * size_p, size_p)
    state[...] = dot((x * tail).T, writes, precision=highest)
    half = heads * size_p // 2
    logs = log_rows(last)
    mine[0:half, :] = state[pl.ds(pl.multiple_of(core * half, half), half), :].astype(bf16)
    mine[half : half + 16, :] = logs
    theirs[0:half, :] = state[pl.ds(pl.multiple_of((1 - core) * half, half), half), :].astype(bf16)
    theirs[half : half + 16, :] = logs


def chip_kernel(size_p, place, mine, other, copies):
    half = mine.shape[0] - 16
    core = place[2]
    first = core * (half // size_p)
    early = core == 0
    log_mine, log_other = log_row(mine, half), log_row(other, half)
    value_mine, value_other = mine[0:half].astype(f32), other[0:half].astype(f32)
    log_late = jnp.where(early, log_other, log_mine)
    value_early = jnp.where(early, value_mine, value_other)
    value_late = jnp.where(early, value_other, value_mine)
    grown = jnp.exp(column(log_late, half, size_p, first)) * value_early + value_late
    value = grown.astype(bf16)
    logs = log_rows(log_mine + log_other)
    for i in range(copies.shape[0]):
        copies[i, 0:half, :] = value
        copies[i, half : half + 16, :] = logs


def prefix_kernel(size_p, place, gathered, mine, other, keep, send):
    half = mine.shape[0] - 16
    core, chip = place[2], place[3]
    first = core * (half // size_p)
    early = core == 0
    state = jnp.zeros((half, mine.shape[1]), f32)
    for i in range(gathered.shape[0] - 1):
        grow = jnp.exp(column(log_row(gathered.at[i], half), half, size_p, first))
        state = jnp.where(i < chip, grow * state + gathered[i, 0:half, :].astype(f32), state)
    log_early = jnp.where(early, log_row(mine, half), log_row(other, half))
    value_early = jnp.where(early, mine[0:half].astype(f32), other[0:half].astype(f32))
    later = jnp.exp(column(log_early, half, size_p, first)) * state + value_early
    keep[...] = jnp.where(early, state, later)
    send[...] = jnp.where(early, later, state).astype(bf16)


def scan_kernel(heads, size_p, block, normed, gate_weight, x_in, writes_in, reads_in, cums_in, step_in, small, result, opened):
    rows = x_in.shape[0]
    width = heads * size_p
    opened[...] = silu(dot(normed[...], gate_weight[...]))
    lower = iota((block, block), 0) >= iota((block, block), 1)
    skip = spread(small[0:8, :], width, size_p)[2:3]
    state = None
    base = None
    for b in range(rows // block):
        span = slice(b * block, (b + 1) * block)
        x, writes, reads = x_in[span, :], writes_in[span, :], reads_in[span, :]
        cums, step = cums_in[span, :], step_in[span, :]
        cums_t, step_t = cums.T, step.T
        scores = dot(reads, writes, ((1,), (1,)), highest)
        made = []
        for h in range(heads):
            gap = cums[:, h : h + 1] - cums_t[h : h + 1, :]
            mixing = jnp.exp(jnp.where(lower, gap, -jnp.inf)) * scores * step_t[h : h + 1, :]
            made.append(dot(mixing, x[:, h * size_p : (h + 1) * size_p], precision=highest))
        y = jnp.concatenate(made, axis=1) + skip * x
        if state is not None:
            carried = dot(reads, state, ((1,), (1,)), highest)
            y = y + spread(jnp.exp(cums - base), width, size_p) * carried
        result[span, :] = y
        if (b + 1) * block < rows:
            last = cums[block - 1 : block, :]
            tail = spread(jnp.exp(last - cums) * step, width, size_p)
            fresh = dot((x * tail).T, writes, precision=highest)
            if state is not None:
                grow = jnp.exp(column(last - base, width, size_p, 0))
                fresh = grow * state + fresh
            state, base = fresh, last


def finish_kernel(heads, size_p, place, result, opened, reads, cums, keep, other, out_gain, out_weight, *refs):
    shares, state = refs[:RING], refs[RING]
    rows, width = result.shape
    own = shares[0].shape[1]
    half = width // 2
    side, turn, core = place[0], place[1], place[2]
    state[pl.ds(pl.multiple_of(core * half, half), half), :] = keep[...]
    state[pl.ds(pl.multiple_of((1 - core) * half, half), half), :] = other[...].astype(f32)
    carried = dot(reads[...], state[...], ((1,), (1,)), highest)
    y = result[...] + spread(jnp.exp(cums[...]), width, size_p) * carried
    g = y * opened[...]
    same = (iota((width, width), 0) // size_p == iota((width, width), 1) // size_p).astype(f32)
    mean = dot(g * g, same, precision=highest) / size_p
    ynorm = (g * lax.rsqrt(mean + eps) * out_gain[...]).astype(bf16)
    for k in range(RING):
        for j in range(SIDE):
            head = lax.rem(side + j, SIDE) * RING + lax.rem(turn + k, RING)
            spot = pl.multiple_of(head * own, own)
            shares[k][j * rows : (j + 1) * rows, :] = dot(ynorm, out_weight[:, pl.ds(spot, own)]).astype(bf16)


def on_chip(kernel, outs, args, place=None, scratch=(), flops=0, transcendentals=0):
    specs = [pl.BlockSpec(memory_space=pltpu.VMEM)] * len(args)
    if place is not None:
        specs = [pl.BlockSpec(memory_space=pltpu.SMEM)] + specs
        args = [place] + list(args)
    moved = sum(a.size * a.dtype.itemsize for a in list(args) + list(outs))
    return pl.pallas_call(
        kernel,
        out_shape=outs,
        in_specs=specs,
        out_specs=[pl.BlockSpec(memory_space=pltpu.VMEM)] * len(outs),
        scratch_shapes=scratch,
        cost_estimate=pl.CostEstimate(flops=flops, bytes_accessed=moved, transcendentals=transcendentals),
        compiler_params=pltpu.CompilerParams(vmem_limit_bytes=VMEM_BYTES),
    )(*args)


def shape(dims, kind=f32):
    return jax.ShapeDtypeStruct(dims, kind)


def to_turn(block, step):
    route = [(i, i // RING * RING + (i + step) % RING) for i in range(SIDE * RING)]
    return lax.ppermute(block, "head", route)


def to_side(block):
    return lax.ppermute(block, "head", [(i, (i + RING) % (SIDE * RING)) for i in range(SIDE * RING)])


def to_core(block):
    return lax.ppermute(block, "section", [(i, i ^ 1) for i in range(lax.axis_size("section"))])


def gather_ring(block):
    found = {0: block}
    rows = block.shape[0] // 2
    for k in range(1, RING // 2):
        found[k] = to_turn(found[k - 1], -1)
        found[RING - k] = to_turn(found[(RING - k + 1) % RING], 1)
    k = RING // 2
    upper = to_turn(found[k - 1][:rows], -1)
    under = to_turn(found[k + 1][rows:], 1)
    found[k] = jnp.concatenate([upper, under], 0)
    return [found[k] for k in range(RING)]


def add(a, b):
    return (a.astype(f32) + b.astype(f32)).astype(bf16)


def reduce_ring(shares):
    rows = shares[0].shape[0] // 2
    far = RING // 2
    up = to_turn(shares[far][:rows], 1)
    down = to_turn(shares[far][rows:], -1)
    near, back = shares[far - 1], shares[far + 1]
    up = jnp.concatenate([add(up, near[:rows]), near[rows:]], 0)
    down = jnp.concatenate([back[:rows], add(down, back[rows:])], 0)
    for k in range(far - 2, 0, -1):
        up = add(to_turn(up, 1), shares[k])
        down = add(to_turn(down, -1), shares[RING - k])
    return shares[0].astype(f32) + to_turn(up, 1).astype(f32) + to_turn(down, -1).astype(f32)


def local(
    tokens,
    norm_gain,
    x_weight,
    gate_weight,
    dt_weight,
    dt_bias,
    decay_rate,
    skip_gain,
    bc_weight,
    out_gain,
    out_weight,
):
    rows, own = tokens.shape
    heads = decay_rate.shape[0]
    width = x_weight.shape[1]
    size_p = width // heads
    state_n = bc_weight.shape[1] // 2
    groups = lax.axis_size("head")
    sections = lax.axis_size("section")
    model = groups * own
    half = width // 2
    head, section = lax.axis_index("head"), lax.axis_index("section")
    core = section % 2
    place = jnp.stack([head // RING, head % RING, core, section // 2]).astype(jnp.int32)

    piece = lax.dynamic_slice_in_dim(bc_weight, core * state_n, state_n, 1)
    bc_one = lax.all_to_all(jnp.broadcast_to(piece[None], (groups, own, state_n)), "head", 0, 0)
    bc_one = bc_one.reshape(model, state_n)
    bc_two = to_core(bc_one)
    both = jnp.concatenate([tokens, to_side(tokens)], 0)
    blocks = gather_ring(both)

    small = jnp.zeros((8, 128), f32)
    small = small.at[0, :heads].set(dt_bias).at[1, :heads].set(decay_rate).at[2, :heads].set(skip_gain)
    dt_wide = jnp.pad(dt_weight, ((0, 0), (0, 128 - heads)))
    normed, x, writes, reads, cums, step, mine, theirs = on_chip(
        functools.partial(project_kernel, heads, size_p),
        [
            shape((rows, model), bf16),
            shape((rows, width)),
            shape((rows, state_n)),
            shape((rows, state_n)),
            shape((rows, 128)),
            shape((rows, 128)),
            shape((half + 16, state_n), bf16),
            shape((half + 16, state_n), bf16),
        ],
        [*blocks, norm_gain.reshape(groups, own), x_weight, dt_wide, bc_one, bc_two, small],
        place,
        [pltpu.VMEM((width, state_n), f32)],
        flops=2 * rows * model * (width + 3 * 128),
    )
    result, opened = on_chip(
        functools.partial(scan_kernel, heads, size_p, 256),
        [shape((rows, width)), shape((rows, width))],
        [normed, gate_weight, x, writes, reads, cums, step, small],
        flops=2 * rows * model * width + 12 * rows * 256 * (width + 3 * state_n),
        transcendentals=heads * rows * 256,
    )
    other = to_core(theirs)
    copies = on_chip(
        functools.partial(chip_kernel, size_p),
        [shape((sections // 2, half + 16, state_n), bf16)],
        [mine, other],
        place,
    )[0]
    chips = [list(range(c, sections, 2)) for c in range(2)]
    gathered = lax.all_to_all(copies, "section", 0, 0, axis_index_groups=chips)
    keep, send = on_chip(
        functools.partial(prefix_kernel, size_p),
        [shape((half, state_n)), shape((half, state_n), bf16)],
        [gathered, mine, other],
        place,
    )
    rest = to_core(send)
    shares = on_chip(
        functools.partial(finish_kernel, heads, size_p),
        [shape((SIDE * rows, own), bf16)] * RING,
        [result, opened, reads, cums, keep, rest, out_gain.reshape(1, width), out_weight],
        place,
        [pltpu.VMEM((width, state_n), f32)],
        flops=2 * rows * model * width,
    )
    summed = reduce_ring(shares)
    return tokens.astype(f32) + summed[:rows] + to_side(summed[rows:].astype(bf16)).astype(f32)


def solution(mesh):
    return jax.shard_map(
        local,
        mesh=mesh,
        in_specs=(
            P("section", "head"),
            P(),
            P(None, "head"),
            P(None, "head"),
            P(None, "head"),
            P("head"),
            P("head"),
            P("head"),
            P("head", None),
            P("head"),
            P("head", None),
        ),
        out_specs=P("section", "head"),
        check_vma=False,
    )
```

```python
import functools

import jax
import jax.numpy as jnp
from jax import lax
from jax.experimental import pallas as pl
from jax.experimental.pallas import tpu as pltpu
from jax.sharding import PartitionSpec as P

eps = 1e-05
highest = lax.Precision.HIGHEST
RING = 8
SIDE = 2
f32 = jnp.float32
bf16 = jnp.bfloat16
VMEM_BYTES = 40 * 1024 * 1024


def dot(a, b, dims=((1,), (0,)), precision=None):
    return lax.dot_general(a, b, (dims, ((), ())), precision=precision, preferred_element_type=f32)


def silu(v):
    return v / (1.0 + jnp.exp(-v))


def softplus(v):
    return jnp.maximum(v, 0.0) + jnp.log1p(jnp.exp(-jnp.abs(v)))


def iota(shape, dim):
    return lax.broadcasted_iota(jnp.int32, shape, dim)


def split(v):
    high = v.astype(bf16)
    return high, (v - high.astype(f32)).astype(bf16)


def dot_pair(a, exact, dims=((1,), (0,))):
    high, low = split(a)
    return dot(high, exact, dims) + dot(low, exact, dims)


def dot_three(a, b, dims=((1,), (0,))):
    a_high, a_low = split(a)
    b_high, b_low = split(b)
    return dot(a_high, b_high, dims) + (dot(a_high, b_low, dims) + dot(a_low, b_high, dims))


def running_sum(v):
    rows = v.shape[0]
    lower = (iota((rows, rows), 0) >= iota((rows, rows), 1)).astype(bf16)
    high, rest = split(v)
    left = v - high.astype(f32)
    middle = rest
    low = (left - middle.astype(f32)).astype(bf16)
    return dot(lower, high) + (dot(lower, middle) + dot(lower, low))


def spread(heads_on_lanes, width, size_p):
    lanes = heads_on_lanes.shape[1]
    pick = (iota((lanes, width), 1) // size_p == iota((lanes, width), 0)).astype(bf16)
    return dot_pair(heads_on_lanes, pick)


def lanes_of(row, scratch):
    scratch[...] = jnp.zeros_like(scratch)
    scratch[0:1, 0 : row.shape[1]] = row[...]
    return scratch[0:1, :]


def column(row, rows, size_p, first):
    lanes = row.shape[1]
    mine = iota((rows, lanes), 1) == iota((rows, lanes), 0) // size_p + first
    return jnp.sum(jnp.where(mine, row, 0.0), axis=1, keepdims=True)


def log_rows(row):
    high = row.astype(bf16).astype(f32)
    low = row - high
    return jnp.concatenate([high, low, jnp.zeros((14, row.shape[1]), f32)], 0).astype(bf16)


def log_row(ref, half):
    tail = ref[half : half + 16].astype(f32)
    return tail[0:1] + tail[1:2]


def norm_kernel(rows, place, *refs):
    blocks = refs[:RING]
    gain, normed, bc_half = refs[RING:]
    own = blocks[0].shape[1]
    side, turn = place[0], place[1]
    piece = blocks[0].shape[0] // SIDE

    def parts():
        for k in range(RING):
            for j in range(SIDE):
                head = lax.rem(side + j, SIDE) * RING + lax.rem(turn + k, RING)
                yield blocks[k], j * piece, head

    squares = jnp.zeros((rows, own), f32)
    for block, at, _ in parts():
        value = block[at : at + rows, :].astype(f32)
        squares = squares + value * value
    mean = jnp.sum(squares, axis=1, keepdims=True) / (RING * SIDE * own)
    scale = lax.rsqrt(mean + eps)
    for block, at, head in parts():
        value = block[at : at + rows, :].astype(f32)
        spot = pl.multiple_of(head * own, own)
        normed[:, pl.ds(spot, own)] = (value * scale * gain[pl.ds(head, 1), :]).astype(bf16)
        bc_half[pl.ds(spot, own), :] = block[at + rows : at + piece, :]


def project_kernel(heads, size_p, normed, x_weight, dt_weight, bias, rate, x_out, tail_out, cums_out, step_out, wide, line):
    rows = normed.shape[0]
    wide[...] = jnp.zeros_like(wide)
    wide[0:heads, :] = dt_weight[...]
    whole = normed[...]
    step = softplus(dot(whole, wide[...], ((1,), (1,))) + lanes_of(bias, line))
    decay = -lanes_of(rate, line) * step
    cums = running_sum(decay)
    x = silu(dot(whole, x_weight[...]))
    last = cums[rows - 1 : rows, :]
    tail = spread(jnp.exp(last - cums) * step, heads * size_p, size_p)
    x_out[...] = x
    tail_out[...] = x * tail
    cums_out[...] = cums
    step_out[...] = step


def state_kernel(place, normed, tailed, bc_one, bc_two, cums, writes_out, mine, theirs, state):
    core = place[2]
    rows, width = tailed.shape
    weight = jnp.where(core == 0, bc_one[...], bc_two[...])
    writes = dot(normed[...], weight)
    writes_out[...] = writes
    state[...] = dot_three(tailed[...].T, writes)
    half = width // 2
    logs = log_rows(cums[rows - 1 : rows, :])
    mine[0:half, :] = state[pl.ds(pl.multiple_of(core * half, half), half), :].astype(bf16)
    mine[half : half + 16, :] = logs
    theirs[0:half, :] = state[pl.ds(pl.multiple_of((1 - core) * half, half), half), :].astype(bf16)
    theirs[half : half + 16, :] = logs


def chip_kernel(size_p, place, mine, other, copies):
    half = mine.shape[0] - 16
    core = place[2]
    first = core * (half // size_p)
    early = core == 0
    log_mine, log_other = log_row(mine, half), log_row(other, half)
    value_mine, value_other = mine[0:half].astype(f32), other[0:half].astype(f32)
    log_late = jnp.where(early, log_other, log_mine)
    value_early = jnp.where(early, value_mine, value_other)
    value_late = jnp.where(early, value_other, value_mine)
    grown = jnp.exp(column(log_late, half, size_p, first)) * value_early + value_late
    value = grown.astype(bf16)
    logs = log_rows(log_mine + log_other)
    for i in range(copies.shape[0]):
        copies[i, 0:half, :] = value
        copies[i, half : half + 16, :] = logs


def prefix_kernel(size_p, place, gathered, mine, other, after, keep, send):
    half = mine.shape[0] - 16
    core, chip = place[2], place[3]
    first = core * (half // size_p)
    early = core == 0
    state = jnp.zeros((half, mine.shape[1]), f32)
    for i in range(gathered.shape[0] - 1):
        grow = jnp.exp(column(log_row(gathered.at[i], half), half, size_p, first))
        state = jnp.where(i < chip, grow * state + gathered[i, 0:half, :].astype(f32), state)
    log_early = jnp.where(early, log_row(mine, half), log_row(other, half))
    value_early = jnp.where(early, mine[0:half].astype(f32), other[0:half].astype(f32))
    later = jnp.exp(column(log_early, half, size_p, first)) * state + value_early
    keep[...] = jnp.where(early, state, later)
    send[...] = jnp.where(early, later, state).astype(bf16)


def scan_kernel(heads, size_p, block, place, normed, gate_weight, bc_one, bc_two, x_in, writes_in, cums_in, step_in, gain, *refs):
    result, opened, reads_out, line = refs
    rows = x_in.shape[0]
    width = heads * size_p
    weight = jnp.where(place[2] == 0, bc_two[...], bc_one[...])
    reads_out[...] = dot(normed[...], weight)
    opened[...] = silu(dot(normed[...], gate_weight[...]))
    lower = iota((block, block), 0) >= iota((block, block), 1)
    skip = spread(lanes_of(gain, line) + jnp.zeros((8, line.shape[1]), f32), width, size_p)[0:1]
    state = None
    base = None
    for b in range(rows // block):
        span = slice(b * block, (b + 1) * block)
        x, writes, reads = x_in[span, :], writes_in[span, :], reads_out[span, :]
        cums, step = cums_in[span, :], step_in[span, :]
        cums_t, step_t = cums.T, step.T
        scores = dot_three(reads, writes, ((1,), (1,)))
        made = []
        for h in range(heads):
            gap = cums[:, h : h + 1] - cums_t[h : h + 1, :]
            mixing = jnp.exp(jnp.where(lower, gap, -jnp.inf)) * scores * step_t[h : h + 1, :]
            made.append(dot_three(mixing, x[:, h * size_p : (h + 1) * size_p]))
        y = jnp.concatenate(made, axis=1) + skip * x
        if state is not None:
            carried = dot_three(reads, state, ((1,), (1,)))
            y = y + spread(jnp.exp(cums - base), width, size_p) * carried
        result[span, :] = y
        if (b + 1) * block < rows:
            last = cums[block - 1 : block, :]
            tail = spread(jnp.exp(last - cums) * step, width, size_p)
            fresh = dot_three((x * tail).T, writes)
            if state is not None:
                fresh = jnp.exp(column(last - base, width, size_p, 0)) * state + fresh
            state, base = fresh, last


def finish_kernel(heads, size_p, place, result, opened, reads, cums, keep, other, out_gain, out_weight, *refs):
    shares, state = refs[:RING], refs[RING]
    rows, width = result.shape
    own = shares[0].shape[1]
    half = width // 2
    side, turn, core = place[0], place[1], place[2]
    state[pl.ds(pl.multiple_of(core * half, half), half), :] = keep[...]
    state[pl.ds(pl.multiple_of((1 - core) * half, half), half), :] = other[...].astype(f32)
    carried = dot_pair(reads[...], state[...].astype(bf16), ((1,), (1,)))
    y = result[...] + spread(jnp.exp(cums[...]), width, size_p) * carried
    g = y * opened[...]
    same = (iota((width, width), 0) // size_p == iota((width, width), 1) // size_p).astype(bf16)
    mean = dot_pair(g * g, same) / size_p
    ynorm = (g * lax.rsqrt(mean + eps) * out_gain[...]).astype(bf16)
    for k in range(RING):
        for j in range(SIDE):
            head = lax.rem(side + j, SIDE) * RING + lax.rem(turn + k, RING)
            spot = pl.multiple_of(head * own, own)
            shares[k][j * rows : (j + 1) * rows, :] = dot(ynorm, out_weight[:, pl.ds(spot, own)]).astype(bf16)


def on_chip(kernel, outs, args, place=None, scratch=(), flops=0, transcendentals=0, whole=()):
    specs = [pl.BlockSpec(memory_space=pl.ANY if i in whole else pltpu.VMEM) for i in range(len(args))]
    if place is not None:
        specs = [pl.BlockSpec(memory_space=pltpu.SMEM)] + specs
        args = [place] + list(args)
    moved = sum(a.size * a.dtype.itemsize for a in list(args) + list(outs))
    return pl.pallas_call(
        kernel,
        out_shape=outs,
        in_specs=specs,
        out_specs=[pl.BlockSpec(memory_space=pltpu.VMEM)] * len(outs),
        scratch_shapes=scratch,
        cost_estimate=pl.CostEstimate(flops=flops, bytes_accessed=moved, transcendentals=transcendentals),
        compiler_params=pltpu.CompilerParams(vmem_limit_bytes=VMEM_BYTES),
    )(*args)


def shape(dims, kind=f32):
    return jax.ShapeDtypeStruct(dims, kind)


def to_turn(block, step):
    route = [(i, i // RING * RING + (i + step) % RING) for i in range(SIDE * RING)]
    return lax.ppermute(block, "head", route)


def to_side(block):
    return lax.ppermute(block, "head", [(i, (i + RING) % (SIDE * RING)) for i in range(SIDE * RING)])


def to_core(block):
    return lax.ppermute(block, "section", [(i, i ^ 1) for i in range(lax.axis_size("section"))])


def gather_ring(block):
    found = {0: block}
    for k in range(1, RING // 2):
        found[k] = to_turn(found[k - 1], -1)
        found[RING - k] = to_turn(found[(RING - k + 1) % RING], 1)
    found[RING // 2] = to_turn(found[RING // 2 - 1], -1)
    return [found[k] for k in range(RING)]


def add(a, b):
    return (a.astype(f32) + b.astype(f32)).astype(bf16)


def reduce_ring(shares):
    far = RING // 2
    up = to_turn(shares[far], 1)
    down = None
    for k in range(far - 1, 0, -1):
        back = shares[RING - k]
        up = to_turn(add(up, shares[k]), 1)
        down = to_turn(back if down is None else add(down, back), -1)
    return shares[0].astype(f32) + up.astype(f32) + down.astype(f32)


def local(
    tokens,
    norm_gain,
    x_weight,
    gate_weight,
    dt_weight,
    dt_bias,
    decay_rate,
    skip_gain,
    bc_weight,
    out_gain,
    out_weight,
):
    rows, own = tokens.shape
    heads = decay_rate.shape[0]
    width = x_weight.shape[1]
    size_p = width // heads
    state_n = bc_weight.shape[1] // 2
    groups = lax.axis_size("head")
    sections = lax.axis_size("section")
    model = groups * own
    half = width // 2
    head, section = lax.axis_index("head"), lax.axis_index("section")
    core = section % 2
    place = jnp.stack([head // RING, head % RING, core, section // 2]).astype(jnp.int32)

    piece = lax.dynamic_slice_in_dim(bc_weight, core * state_n, state_n, 1)
    packed = jnp.concatenate([tokens, piece], 0)
    blocks = gather_ring(jnp.concatenate([packed, to_side(packed)], 0))
    normed, bc_one = on_chip(
        functools.partial(norm_kernel, rows),
        [shape((rows, model), bf16), shape((model, state_n), bf16)],
        [*blocks, norm_gain.reshape(groups, own)],
        place,
    )
    bc_two = to_core(bc_one)
    x, tailed, cums, step = on_chip(
        functools.partial(project_kernel, heads, size_p),
        [shape((rows, width)), shape((rows, width)), shape((rows, 128)), shape((rows, 128))],
        [normed, x_weight, dt_weight.T, dt_bias.reshape(1, heads), decay_rate.reshape(1, heads)],
        scratch=[pltpu.VMEM((128, model), bf16), pltpu.VMEM((8, 128), f32)],
        flops=2 * rows * model * (width + 128),
    )
    writes, mine, theirs = on_chip(
        state_kernel,
        [shape((rows, state_n)), shape((half + 16, state_n), bf16), shape((half + 16, state_n), bf16)],
        [normed, tailed, bc_one, bc_two, cums],
        place,
        [pltpu.VMEM((width, state_n), f32)],
        flops=2 * rows * model * state_n,
    )
    result, opened, reads = on_chip(
        functools.partial(scan_kernel, heads, size_p, 256),
        [shape((rows, width)), shape((rows, width)), shape((rows, state_n))],
        [normed, gate_weight, bc_one, bc_two, x, writes, cums, step, skip_gain.reshape(1, heads)],
        place,
        [pltpu.VMEM((8, 128), f32)],
        flops=2 * rows * model * (width + state_n) + 12 * rows * 256 * (width + 3 * state_n),
        transcendentals=heads * rows * 256,
    )
    other = to_core(theirs)
    copies = on_chip(
        functools.partial(chip_kernel, size_p),
        [shape((sections // 2, half + 16, state_n), bf16)],
        [mine, other],
        place,
    )[0]
    chips = [list(range(c, sections, 2)) for c in range(2)]
    gathered = lax.all_to_all(copies, "section", 0, 0, axis_index_groups=chips)
    keep, send = on_chip(
        functools.partial(prefix_kernel, size_p),
        [shape((half, state_n)), shape((half, state_n), bf16)],
        [gathered, mine, other, result],
        place,
        whole=(3,),
    )
    rest = to_core(send)
    shares = on_chip(
        functools.partial(finish_kernel, heads, size_p),
        [shape((SIDE * rows, own), bf16)] * RING,
        [result, opened, reads, cums, keep, rest, out_gain.reshape(1, width), out_weight],
        place,
        [pltpu.VMEM((width, state_n), f32)],
        flops=2 * rows * model * width,
    )
    summed = reduce_ring(shares)
    return tokens.astype(f32) + summed[:rows] + to_side(summed[rows:].astype(bf16)).astype(f32)


def solution(mesh):
    return jax.shard_map(
        local,
        mesh=mesh,
        in_specs=(
            P("section", "head"),
            P(),
            P(None, "head"),
            P(None, "head"),
            P(None, "head"),
            P("head"),
            P("head"),
            P("head"),
            P("head", None),
            P("head"),
            P("head", None),
        ),
        out_specs=P("section", "head"),
        check_vma=False,
    )
```

```python
import functools

import jax
import jax.numpy as jnp
from jax import lax
from jax.experimental import pallas as pl
from jax.experimental.pallas import tpu as pltpu
from jax.sharding import PartitionSpec as P

eps = 1e-05
highest = lax.Precision.HIGHEST
RING = 8
SIDE = 2
ROW = 8
f32 = jnp.float32
bf16 = jnp.bfloat16
VMEM_BYTES = 24 * 1024 * 1024


def dot(a, b, dims=((1,), (0,)), precision=None):
    return lax.dot_general(a, b, (dims, ((), ())), precision=precision, preferred_element_type=f32)


def silu(v):
    return v / (1.0 + jnp.exp(-v))


def softplus(v):
    return jnp.maximum(v, 0.0) + jnp.log1p(jnp.exp(-jnp.abs(v)))


def iota(shape, dim):
    return lax.broadcasted_iota(jnp.int32, shape, dim)


def split(v):
    high = v.astype(bf16)
    return high, (v - high.astype(f32)).astype(bf16)


def dot_pair(a, exact, dims=((1,), (0,))):
    high, low = split(a)
    return dot(high, exact, dims) + dot(low, exact, dims)


def dot_three(a, b, dims=((1,), (0,))):
    a_high, a_low = split(a)
    b_high, b_low = split(b)
    return dot(a_high, b_high, dims) + (dot(a_high, b_low, dims) + dot(a_low, b_high, dims))


def running_sum(v):
    rows = v.shape[0]
    lower = (iota((rows, rows), 0) >= iota((rows, rows), 1)).astype(bf16)
    high, rest = split(v)
    left = v - high.astype(f32)
    middle = rest
    low = (left - middle.astype(f32)).astype(bf16)
    return dot(lower, high) + (dot(lower, middle) + dot(lower, low))


def spread(heads_on_lanes, width, size_p):
    lanes = heads_on_lanes.shape[1]
    pick = (iota((lanes, width), 1) // size_p == iota((lanes, width), 0)).astype(bf16)
    return dot_pair(heads_on_lanes, pick)


def lanes_of(row, scratch):
    scratch[...] = jnp.zeros_like(scratch)
    scratch[0:1, 0 : row.shape[1]] = row[...]
    return scratch[0:1, :]


def column(row, rows, size_p, first):
    lanes = row.shape[1]
    mine = iota((rows, lanes), 1) == iota((rows, lanes), 0) // size_p + first
    return jnp.sum(jnp.where(mine, row, 0.0), axis=1, keepdims=True)


def log_rows(row):
    high = row.astype(bf16).astype(f32)
    low = row - high
    return jnp.concatenate([high, low, jnp.zeros((14, row.shape[1]), f32)], 0).astype(bf16)


def log_row(ref, half):
    tail = ref[half : half + 16].astype(f32)
    return tail[0:1] + tail[1:2]


def norm_kernel(rows, place, *refs):
    blocks = refs[:RING]
    gain, normed, bc_half = refs[RING:]
    own = blocks[0].shape[1]
    side, turn = place[0], place[1]
    piece = blocks[0].shape[0] // SIDE

    def parts():
        for k in range(RING):
            for j in range(SIDE):
                head = lax.rem(side + j, SIDE) * RING + lax.rem(turn + k, RING)
                yield blocks[k], j * piece, head

    squares = jnp.zeros((rows, own), f32)
    for block, at, _ in parts():
        value = block[at : at + rows, :].astype(f32)
        squares = squares + value * value
    mean = jnp.sum(squares, axis=1, keepdims=True) / (RING * SIDE * own)
    scale = lax.rsqrt(mean + eps)
    for block, at, head in parts():
        value = block[at : at + rows, :].astype(f32)
        spot = pl.multiple_of(head * own, own)
        normed[:, pl.ds(spot, own)] = (value * scale * gain[pl.ds(head, 1), :]).astype(bf16)
        bc_half[pl.ds(spot, own), :] = block[at + rows : at + piece, :]


def project_kernel(heads, size_p, normed, x_weight, dt_weight, bias, rate, x_out, tail_out, cums_out, step_out, wide, line):
    rows = normed.shape[0]
    wide[...] = jnp.zeros_like(wide)
    wide[0:heads, :] = dt_weight[...]
    whole = normed[...]
    step = softplus(dot(whole, wide[...], ((1,), (1,))) + lanes_of(bias, line))
    decay = -lanes_of(rate, line) * step
    cums = running_sum(decay)
    x = silu(dot(whole, x_weight[...]))
    last = cums[rows - 1 : rows, :]
    tail = spread(jnp.exp(last - cums) * step, heads * size_p, size_p)
    x_out[...] = x
    tail_out[...] = x * tail
    cums_out[...] = cums
    step_out[...] = step


def state_kernel(place, normed, tailed, bc_one, bc_two, cums, writes_out, slots, state):
    core = place[2]
    rows, width = tailed.shape
    weight = jnp.where(core == 0, bc_one[...], bc_two[...])
    writes = dot(normed[...], weight)
    writes_out[...] = writes
    state[...] = dot_three(tailed[...].T, writes)
    half = width // 2
    logs = log_rows(cums[rows - 1 : rows, :])
    for i in range(slots.shape[0]):
        at = i % 2 * half
        slots[i, 0:half, :] = state[at : at + half, :].astype(bf16)
        slots[i, half : half + 16, :] = logs


def row_kernel(size_p, place, gathered, copies, own_out, pair_out, logs_out):
    half = gathered.shape[1] - 16
    core, spot = place[2], place[3]
    first = core * (half // size_p)
    pair = spot + 1 - 2 * core
    state = jnp.zeros((half, gathered.shape[2]), f32)
    log = jnp.zeros((1, gathered.shape[2]), f32)
    own, other, own_log, other_log = state, state, log, log
    for i in range(gathered.shape[0]):
        own, own_log = jnp.where(i == spot, state, own), jnp.where(i == spot, log, own_log)
        other, other_log = jnp.where(i == pair, state, other), jnp.where(i == pair, log, other_log)
        here = log_row(gathered.at[i], half)
        state = jnp.exp(column(here, half, size_p, first)) * state + gathered[i, 0:half, :].astype(f32)
        log = log + here
    own_out[...] = own
    pair_out[...] = other
    logs_out[0:1, :] = own_log
    logs_out[1:2, :] = other_log
    value, logs = state.astype(bf16), log_rows(log)
    for i in range(copies.shape[0]):
        copies[i, 0:half, :] = value
        copies[i, half : half + 16, :] = logs


def prefix_kernel(size_p, place, gathered, own, pair, logs, keep, send):
    half = own.shape[0]
    core, row = place[2], place[4]
    first = core * (half // size_p)
    state = jnp.zeros((half, own.shape[1]), f32)
    for i in range(gathered.shape[0] - 1):
        grow = jnp.exp(column(log_row(gathered.at[i], half), half, size_p, first))
        state = jnp.where(i < row, grow * state + gathered[i, 0:half, :].astype(f32), state)
    keep[...] = jnp.exp(column(logs[0:1, :], half, size_p, first)) * state + own[...]
    later = jnp.exp(column(logs[1:2, :], half, size_p, first)) * state + pair[...]
    send[...] = later.astype(bf16)


def scan_kernel(heads, size_p, block, place, normed, gate_weight, bc_one, bc_two, x_in, writes_in, cums_in, step_in, gain, *refs):
    result, opened, reads_out, line = refs
    rows = x_in.shape[0]
    width = heads * size_p
    weight = jnp.where(place[2] == 0, bc_two[...], bc_one[...])
    reads_out[...] = dot(normed[...], weight)
    opened[...] = silu(dot(normed[...], gate_weight[...]))
    lower = iota((block, block), 0) >= iota((block, block), 1)
    skip = spread(lanes_of(gain, line) + jnp.zeros((8, line.shape[1]), f32), width, size_p)[0:1]
    state = None
    base = None
    for b in range(rows // block):
        span = slice(b * block, (b + 1) * block)
        x, writes, reads = x_in[span, :], writes_in[span, :], reads_out[span, :]
        cums, step = cums_in[span, :], step_in[span, :]
        cums_t, step_t = cums.T, step.T
        scores = dot_three(reads, writes, ((1,), (1,)))
        made = []
        for h in range(heads):
            gap = cums[:, h : h + 1] - cums_t[h : h + 1, :]
            mixing = jnp.exp(jnp.where(lower, gap, -jnp.inf)) * scores * step_t[h : h + 1, :]
            made.append(dot(mixing.astype(bf16), x[:, h * size_p : (h + 1) * size_p].astype(bf16)))
        y = jnp.concatenate(made, axis=1) + skip * x
        if state is not None:
            carried = dot_three(reads, state, ((1,), (1,)))
            y = y + spread(jnp.exp(cums - base), width, size_p) * carried
        result[span, :] = y
        if (b + 1) * block < rows:
            last = cums[block - 1 : block, :]
            tail = spread(jnp.exp(last - cums) * step, width, size_p)
            fresh = dot_three((x * tail).T, writes)
            if state is not None:
                fresh = jnp.exp(column(last - base, width, size_p, 0)) * state + fresh
            state, base = fresh, last


def finish_kernel(heads, size_p, place, result, opened, reads, cums, keep, other, out_gain, out_weight, *refs):
    shares, state = refs[:RING], refs[RING]
    rows, width = result.shape
    own = shares[0].shape[1]
    half = width // 2
    side, turn, core = place[0], place[1], place[2]
    state[pl.ds(pl.multiple_of(core * half, half), half), :] = keep[...]
    state[pl.ds(pl.multiple_of((1 - core) * half, half), half), :] = other[...].astype(f32)
    carried = dot_pair(reads[...], state[...].astype(bf16), ((1,), (1,)))
    y = result[...] + spread(jnp.exp(cums[...]), width, size_p) * carried
    g = y * opened[...]
    same = (iota((width, width), 0) // size_p == iota((width, width), 1) // size_p).astype(bf16)
    mean = dot_pair(g * g, same) / size_p
    ynorm = (g * lax.rsqrt(mean + eps) * out_gain[...]).astype(bf16)
    for k in range(RING):
        for j in range(SIDE):
            head = lax.rem(side + j, SIDE) * RING + lax.rem(turn + k, RING)
            spot = pl.multiple_of(head * own, own)
            shares[k][j * rows : (j + 1) * rows, :] = dot(ynorm, out_weight[:, pl.ds(spot, own)]).astype(bf16)


def on_chip(kernel, outs, args, place=None, scratch=(), flops=0, transcendentals=0, whole=()):
    specs = [pl.BlockSpec(memory_space=pl.ANY if i in whole else pltpu.VMEM) for i in range(len(args))]
    if place is not None:
        specs = [pl.BlockSpec(memory_space=pltpu.SMEM)] + specs
        args = [place] + list(args)
    moved = sum(a.size * a.dtype.itemsize for a in list(args) + list(outs))
    return pl.pallas_call(
        kernel,
        out_shape=outs,
        in_specs=specs,
        out_specs=[pl.BlockSpec(memory_space=pltpu.VMEM)] * len(outs),
        scratch_shapes=scratch,
        cost_estimate=pl.CostEstimate(flops=flops, bytes_accessed=moved, transcendentals=transcendentals),
        compiler_params=pltpu.CompilerParams(vmem_limit_bytes=VMEM_BYTES),
    )(*args)


def shape(dims, kind=f32):
    return jax.ShapeDtypeStruct(dims, kind)


def to_turn(block, step):
    route = [(i, i // RING * RING + (i + step) % RING) for i in range(SIDE * RING)]
    return lax.ppermute(block, "head", route)


def to_side(block):
    return lax.ppermute(block, "head", [(i, (i + RING) % (SIDE * RING)) for i in range(SIDE * RING)])


def to_core(block):
    return lax.ppermute(block, "section", [(i, i ^ 1) for i in range(lax.axis_size("section"))])


def gather_ring(block):
    found = {0: block}
    for k in range(1, RING // 2):
        found[k] = to_turn(found[k - 1], -1)
        found[RING - k] = to_turn(found[(RING - k + 1) % RING], 1)
    found[RING // 2] = to_turn(found[RING // 2 - 1], -1)
    return [found[k] for k in range(RING)]


def add(a, b):
    return (a.astype(f32) + b.astype(f32)).astype(bf16)


def reduce_ring(shares):
    far = RING // 2
    up = to_turn(shares[far], 1)
    down = None
    for k in range(far - 1, 0, -1):
        back = shares[RING - k]
        up = to_turn(add(up, shares[k]), 1)
        down = to_turn(back if down is None else add(down, back), -1)
    return shares[0].astype(f32) + up.astype(f32) + down.astype(f32)


def local(
    tokens,
    norm_gain,
    x_weight,
    gate_weight,
    dt_weight,
    dt_bias,
    decay_rate,
    skip_gain,
    bc_weight,
    out_gain,
    out_weight,
):
    rows, own = tokens.shape
    heads = decay_rate.shape[0]
    width = x_weight.shape[1]
    size_p = width // heads
    state_n = bc_weight.shape[1] // 2
    groups = lax.axis_size("head")
    sections = lax.axis_size("section")
    model = groups * own
    half = width // 2
    head, section = lax.axis_index("head"), lax.axis_index("section")
    core = section % 2
    place = jnp.stack([head // RING, head % RING, core, section % ROW, section // ROW]).astype(jnp.int32)

    piece = lax.dynamic_slice_in_dim(bc_weight, core * state_n, state_n, 1)
    packed = jnp.concatenate([tokens, piece], 0)
    blocks = gather_ring(jnp.concatenate([packed, to_side(packed)], 0))
    normed, bc_one = on_chip(
        functools.partial(norm_kernel, rows),
        [shape((rows, model), bf16), shape((model, state_n), bf16)],
        [*blocks, norm_gain.reshape(groups, own)],
        place,
    )
    bc_two = to_core(bc_one)
    x, tailed, cums, step = on_chip(
        functools.partial(project_kernel, heads, size_p),
        [shape((rows, width)), shape((rows, width)), shape((rows, 128)), shape((rows, 128))],
        [normed, x_weight, dt_weight.T, dt_bias.reshape(1, heads), decay_rate.reshape(1, heads)],
        scratch=[pltpu.VMEM((128, model), bf16), pltpu.VMEM((8, 128), f32)],
        flops=2 * rows * model * (width + 128),
    )
    writes, slots = on_chip(
        state_kernel,
        [shape((rows, state_n)), shape((ROW, half + 16, state_n), bf16)],
        [normed, tailed, bc_one, bc_two, cums],
        place,
        [pltpu.VMEM((width, state_n), f32)],
        flops=2 * rows * model * state_n,
    )
    result, opened, reads = on_chip(
        functools.partial(scan_kernel, heads, size_p, 256),
        [shape((rows, width)), shape((rows, width)), shape((rows, state_n))],
        [normed, gate_weight, bc_one, bc_two, x, writes, cums, step, skip_gain.reshape(1, heads)],
        place,
        [pltpu.VMEM((8, 128), f32)],
        flops=2 * rows * model * (width + state_n) + 12 * rows * 256 * (width + 3 * state_n),
        transcendentals=heads * rows * 256,
    )
    lines = sections // ROW
    by_row = [list(range(r * ROW, (r + 1) * ROW)) for r in range(lines)]
    by_spot = [list(range(p, sections, ROW)) for p in range(ROW)]
    copies, enter_own, enter_pair, logs = on_chip(
        functools.partial(row_kernel, size_p),
        [shape((lines, half + 16, state_n), bf16), shape((half, state_n)), shape((half, state_n)), shape((8, state_n))],
        [lax.all_to_all(slots, "section", 0, 0, axis_index_groups=by_row)],
        place,
    )
    keep, send = on_chip(
        functools.partial(prefix_kernel, size_p),
        [shape((half, state_n)), shape((half, state_n), bf16)],
        [lax.all_to_all(copies, "section", 0, 0, axis_index_groups=by_spot), enter_own, enter_pair, logs],
        place,
    )
    rest = to_core(send)
    shares = on_chip(
        functools.partial(finish_kernel, heads, size_p),
        [shape((SIDE * rows, own), bf16)] * RING,
        [result, opened, reads, cums, keep, rest, out_gain.reshape(1, width), out_weight],
        place,
        [pltpu.VMEM((width, state_n), f32)],
        flops=2 * rows * model * width,
    )
    summed = reduce_ring(shares)
    return tokens.astype(f32) + summed[:rows] + to_side(summed[rows:].astype(bf16)).astype(f32)


def solution(mesh):
    return jax.shard_map(
        local,
        mesh=mesh,
        in_specs=(
            P("section", "head"),
            P(),
            P(None, "head"),
            P(None, "head"),
            P(None, "head"),
            P("head"),
            P("head"),
            P("head"),
            P("head", None),
            P("head"),
            P("head", None),
        ),
        out_specs=P("section", "head"),
        check_vma=False,
    )
```

```python
import functools

import jax
import jax.numpy as jnp
from jax import lax
from jax.experimental import pallas as pl
from jax.experimental.pallas import tpu as pltpu
from jax.sharding import PartitionSpec as P

eps = 1e-05
RING = 8
SIDE = 2
ROW = 8
HEADS = 16
f32 = jnp.float32
bf16 = jnp.bfloat16
VMEM_BYTES = 24 * 1024 * 1024


def dot(a, b, dims=((1,), (0,))):
    return lax.dot_general(a, b, (dims, ((), ())), preferred_element_type=f32)


def silu(v):
    return v / (1.0 + jnp.exp(-v))


def softplus(v):
    return jnp.maximum(v, 0.0) + jnp.log1p(jnp.exp(-jnp.abs(v)))


def iota(shape, dim):
    return lax.broadcasted_iota(jnp.int32, shape, dim)


def split(v):
    high = v.astype(bf16)
    return high, (v - high.astype(f32)).astype(bf16)


def dot_pair(a, exact, dims=((1,), (0,))):
    high, low = split(a)
    return dot(high, exact, dims) + dot(low, exact, dims)


def dot_three(a, b, dims=((1,), (0,))):
    a_high, a_low = split(a)
    b_high, b_low = split(b)
    return dot(a_high, b_high, dims) + (dot(a_high, b_low, dims) + dot(a_low, b_high, dims))


def running_sum(v):
    count = v.shape[1]
    upper = (iota((count, count), 0) <= iota((count, count), 1)).astype(bf16)
    high, middle = split(v)
    low = (v - high.astype(f32) - middle.astype(f32)).astype(bf16)
    return dot(high, upper) + (dot(middle, upper) + dot(low, upper))


def owners(width, size_p):
    return iota((HEADS, width), 1) // size_p == iota((HEADS, width), 0)


def spread(heads_on_lanes, width, size_p):
    return dot_pair(heads_on_lanes, owners(width, size_p).astype(bf16))


def spread_row(heads_on_rows, width, size_p):
    return jnp.sum(jnp.where(owners(width, size_p), heads_on_rows, 0.0), axis=0, keepdims=True)


def stood(row, scratch):
    scratch[...] = jnp.zeros_like(scratch)
    scratch[0:1, 0 : row.shape[1]] = row[...]
    square = iota((HEADS, HEADS), 0) == iota((HEADS, HEADS), 1)
    return jnp.sum(jnp.where(square, scratch[0:1, 0:HEADS], 0.0), axis=1, keepdims=True)


def log_rows(row):
    high = row.astype(bf16).astype(f32)
    low = row - high
    return jnp.concatenate([high, low, jnp.zeros((14, row.shape[1]), f32)], 0).astype(bf16)


def log_row(block):
    tail = block[block.shape[0] - 16 :].astype(f32)
    return tail[0:1] + tail[1:2]


def front_kernel(rows, heads, size_p, place, *refs):
    blocks = refs[:RING]
    (gain, x_weight, dt_weight, bias, rate) = refs[RING : RING + 5]
    (normed, x_out, both_out, cums_out, step_out, slots, bc, wide, line) = refs[RING + 5 :]
    own = blocks[0].shape[1]
    side, turn = place[0], place[1]
    piece = blocks[0].shape[0] // SIDE
    width = heads * size_p
    state_n = own

    def parts():
        for k in range(RING):
            for j in range(SIDE):
                head = lax.rem(side + j, SIDE) * RING + lax.rem(turn + k, RING)
                yield blocks[k], j * piece, head

    squares = jnp.zeros((rows, own), f32)
    for block, at, _ in parts():
        value = block[at : at + rows, :].astype(f32)
        squares = squares + value * value
    mean = jnp.sum(squares, axis=1, keepdims=True) / (RING * SIDE * own)
    scale = lax.rsqrt(mean + eps)
    for block, at, head in parts():
        value = block[at : at + rows, :].astype(f32)
        spot = pl.multiple_of(head * own, own)
        normed[:, pl.ds(spot, own)] = (value * scale * gain[pl.ds(head, 1), :]).astype(bf16)
        bc[pl.ds(spot, own), 0:state_n] = block[at + rows : at + rows + own, :]
        bc[pl.ds(spot, own), state_n : 2 * state_n] = block[at + rows + own : at + piece, :]
    wide[...] = jnp.zeros_like(wide)
    wide[0:heads, :] = dt_weight[...]
    whole = normed[...]
    raw = dot(whole, wide[...], ((1,), (1,))).T[0:HEADS, :]
    step = softplus(raw + stood(bias, line))
    decay = -stood(rate, line) * step
    cums = running_sum(decay)
    last = cums[:, rows - 1 : rows]
    tail = (jnp.exp(last - cums) * step).T
    x = silu(dot(whole, x_weight[...]))
    both = dot(whole, bc[...])
    state = dot_three(both[:, 0:state_n].T, x * spread(tail, width, size_p)).astype(bf16)
    logs = log_rows(spread_row(last, width, size_p))
    half = width // 2
    for i in range(slots.shape[0]):
        at = i % 2 * half
        slots[i, 0:state_n, :] = state[:, at : at + half]
        slots[i, state_n : state_n + 16, :] = logs[:, at : at + half]
    x_out[...] = x
    both_out[...] = both
    cums_out[...] = cums
    step_out[...] = step


def row_kernel(place, gathered, copies, own_out, pair_out, logs_out):
    state_n, half = gathered.shape[1] - 16, gathered.shape[2]
    core, spot = place[2], place[3]
    pair = spot + 1 - 2 * core
    state = jnp.zeros((state_n, half), f32)
    log = jnp.zeros((1, half), f32)
    own, other, own_log, other_log = state, state, log, log
    for i in range(gathered.shape[0]):
        own, own_log = jnp.where(i == spot, state, own), jnp.where(i == spot, log, own_log)
        other, other_log = jnp.where(i == pair, state, other), jnp.where(i == pair, log, other_log)
        here = log_row(gathered[i])
        state = jnp.exp(here) * state + gathered[i, 0:state_n, :].astype(f32)
        log = log + here
    own_out[...] = own
    pair_out[...] = other
    logs_out[0:1, :] = own_log
    logs_out[1:2, :] = other_log
    value, logs = state.astype(bf16), log_rows(log)
    for i in range(copies.shape[0]):
        copies[i, 0:state_n, :] = value
        copies[i, state_n : state_n + 16, :] = logs


def prefix_kernel(place, gathered, own, pair, logs, keep, send):
    state_n = own.shape[0]
    row = place[4]
    state = jnp.zeros(own.shape, f32)
    for i in range(gathered.shape[0] - 1):
        passed = jnp.exp(log_row(gathered[i])) * state + gathered[i, 0:state_n, :].astype(f32)
        state = jnp.where(i < row, passed, state)
    keep[...] = (jnp.exp(logs[0:1, :]) * state + own[...]).astype(bf16)
    send[...] = (jnp.exp(logs[1:2, :]) * state + pair[...]).astype(bf16)


def scan_kernel(heads, size_p, block, normed, gate_weight, x_in, both_in, cums_in, step_in, gain, result, opened, line):
    rows, width = x_in.shape
    state_n = both_in.shape[1] // 2
    opened[...] = silu(dot(normed[...], gate_weight[...]))
    lower = iota((block, block), 0) >= iota((block, block), 1)
    skip = spread_row(stood(gain, line), width, size_p)
    state = None
    base = None
    for b in range(rows // block):
        span = slice(b * block, (b + 1) * block)
        x, writes, reads = x_in[span, :], both_in[span, 0:state_n], both_in[span, state_n:]
        cums_t, step_t = cums_in[:, span], step_in[:, span]
        cums = cums_t.T
        scores = dot_three(reads, writes, ((1,), (1,)))
        made = []
        for h in range(heads):
            gap = cums[:, h : h + 1] - cums_t[h : h + 1, :]
            mixing = jnp.exp(jnp.where(lower, gap, -jnp.inf)) * scores * step_t[h : h + 1, :]
            made.append(dot(mixing.astype(bf16), x[:, h * size_p : (h + 1) * size_p].astype(bf16)))
        y = jnp.concatenate(made, axis=1) + skip * x
        if state is not None:
            y = y + spread(jnp.exp(cums_t - base).T, width, size_p) * dot_three(reads, state)
        result[span, :] = y
        if (b + 1) * block < rows:
            last = cums_t[:, block - 1 : block]
            tail = (jnp.exp(last - cums_t) * step_t).T
            fresh = dot_three(writes.T, x * spread(tail, width, size_p))
            if state is not None:
                fresh = jnp.exp(spread_row(last - base, width, size_p)) * state + fresh
            state, base = fresh, last


def share(ynorm, out_weight, place, k, out):
    rows, own = ynorm.shape[0], out.shape[1]
    for j in range(SIDE):
        head = lax.rem(place[0] + j, SIDE) * RING + lax.rem(place[1] + k, RING)
        spot = pl.multiple_of(head * own, own)
        out[j * rows : (j + 1) * rows, :] = dot(ynorm, out_weight[:, pl.ds(spot, own)]).astype(bf16)


def finish_kernel(size_p, ks, place, result, opened, both, cums, keep, other, out_gain, out_weight, ynorm_out, *shares):
    rows, width = result.shape
    state_n = both.shape[1] // 2
    first = place[2] == 0
    left, right = jnp.where(first, keep[...], other[...]), jnp.where(first, other[...], keep[...])
    state = jnp.concatenate([left, right], axis=1)
    carried = dot_pair(both[:, state_n:], state)
    y = result[...] + spread(jnp.exp(cums[...]).T, width, size_p) * carried
    g = y * opened[...]
    same = (iota((width, width), 0) // size_p == iota((width, width), 1) // size_p).astype(bf16)
    mean = dot_pair(g * g, same) / size_p
    ynorm = (g * lax.rsqrt(mean + eps) * out_gain[...]).astype(bf16)
    ynorm_out[...] = ynorm
    for k, out in zip(ks, shares):
        share(ynorm, out_weight, place, k, out)


def share_kernel(ks, place, ynorm, out_weight, *shares):
    for k, out in zip(ks, shares):
        share(ynorm[...], out_weight, place, k, out)


def on_chip(kernel, outs, args, place=None, scratch=(), flops=0, transcendentals=0, whole=()):
    specs = [pl.BlockSpec(memory_space=pl.ANY if i in whole else pltpu.VMEM) for i in range(len(args))]
    if place is not None:
        specs = [pl.BlockSpec(memory_space=pltpu.SMEM)] + specs
        args = [place] + list(args)
    moved = sum(a.size * a.dtype.itemsize for a in list(args) + list(outs))
    return pl.pallas_call(
        kernel,
        out_shape=outs,
        in_specs=specs,
        out_specs=[pl.BlockSpec(memory_space=pltpu.VMEM)] * len(outs),
        scratch_shapes=scratch,
        cost_estimate=pl.CostEstimate(flops=flops, bytes_accessed=moved, transcendentals=transcendentals),
        compiler_params=pltpu.CompilerParams(vmem_limit_bytes=VMEM_BYTES),
    )(*args)


def shape(dims, kind=f32):
    return jax.ShapeDtypeStruct(dims, kind)


def to_turn(block, step):
    route = [(i, i // RING * RING + (i + step) % RING) for i in range(SIDE * RING)]
    return lax.ppermute(block, "head", route)


def to_side(block):
    return lax.ppermute(block, "head", [(i, (i + RING) % (SIDE * RING)) for i in range(SIDE * RING)])


def to_core(block):
    return lax.ppermute(block, "section", [(i, i ^ 1) for i in range(lax.axis_size("section"))])


def gather_ring(block):
    found = {0: block}
    for k in range(1, RING // 2):
        found[k] = to_turn(found[k - 1], -1)
        found[RING - k] = to_turn(found[(RING - k + 1) % RING], 1)
    found[RING // 2] = to_turn(found[RING // 2 - 1], -1)
    return [found[k] for k in range(RING)]


def add(a, b):
    return (a.astype(f32) + b.astype(f32)).astype(bf16)


def reduce_ring(shares):
    far = RING // 2
    up = to_turn(shares[far], 1)
    down = None
    for k in range(far - 1, 0, -1):
        back = shares[RING - k]
        up = to_turn(add(up, shares[k]), 1)
        down = to_turn(back if down is None else add(down, back), -1)
    return shares[0].astype(f32) + up.astype(f32) + down.astype(f32)


def local(
    tokens,
    norm_gain,
    x_weight,
    gate_weight,
    dt_weight,
    dt_bias,
    decay_rate,
    skip_gain,
    bc_weight,
    out_gain,
    out_weight,
):
    rows, own = tokens.shape
    heads = decay_rate.shape[0]
    width = x_weight.shape[1]
    size_p = width // heads
    state_n = bc_weight.shape[1] // 2
    groups = lax.axis_size("head")
    sections = lax.axis_size("section")
    model = groups * own
    half = width // 2
    head, section = lax.axis_index("head"), lax.axis_index("section")
    place = jnp.stack([head // RING, head % RING, section % 2, section % ROW, section // ROW]).astype(jnp.int32)

    bc = jnp.concatenate([bc_weight[:, :state_n], bc_weight[:, state_n:]], 0)
    blocks = gather_ring(jnp.concatenate([tokens, bc, to_side(tokens), to_side(bc)], 0))
    normed, x, both, cums, step, slots = on_chip(
        functools.partial(front_kernel, rows, heads, size_p),
        [
            shape((rows, model), bf16),
            shape((rows, width)),
            shape((rows, 2 * state_n)),
            shape((HEADS, rows)),
            shape((HEADS, rows)),
            shape((ROW, state_n + 16, half), bf16),
        ],
        [
            *blocks,
            norm_gain.reshape(groups, own),
            x_weight,
            dt_weight.T,
            dt_bias.reshape(1, heads),
            decay_rate.reshape(1, heads),
        ],
        place,
        [pltpu.VMEM((model, 2 * state_n), bf16), pltpu.VMEM((128, model), bf16), pltpu.VMEM((8, 128), f32)],
        flops=2 * rows * model * (width + 2 * state_n + 128),
    )
    result, opened = on_chip(
        functools.partial(scan_kernel, heads, size_p, 256),
        [shape((rows, width)), shape((rows, width))],
        [normed, gate_weight, x, both, cums, step, skip_gain.reshape(1, heads)],
        scratch=[pltpu.VMEM((8, 128), f32)],
        flops=2 * rows * model * width + 12 * rows * 256 * (width + 3 * state_n),
        transcendentals=heads * rows * 256,
    )
    lines = sections // ROW
    by_row = [list(range(r * ROW, (r + 1) * ROW)) for r in range(lines)]
    by_spot = [list(range(p, sections, ROW)) for p in range(ROW)]
    copies, enter_own, enter_pair, logs = on_chip(
        row_kernel,
        [shape((lines, state_n + 16, half), bf16), shape((state_n, half)), shape((state_n, half)), shape((8, half))],
        [lax.all_to_all(slots, "section", 0, 0, axis_index_groups=by_row)],
        place,
    )
    keep, send = on_chip(
        prefix_kernel,
        [shape((state_n, half), bf16), shape((state_n, half), bf16)],
        [lax.all_to_all(copies, "section", 0, 0, axis_index_groups=by_spot), enter_own, enter_pair, logs],
        place,
    )
    rest = to_core(send)
    soon, later = (RING // 2, RING // 2 + 1), tuple(k for k in range(RING) if k // 2 != RING // 4)
    ynorm, *early = on_chip(
        functools.partial(finish_kernel, size_p, soon),
        [shape((rows, width), bf16)] + [shape((SIDE * rows, own), bf16)] * len(soon),
        [result, opened, both, cums, keep, rest, out_gain.reshape(1, width), out_weight],
        place,
        flops=2 * rows * width * (2 * SIDE * own + 4 * width),
    )
    late = on_chip(
        functools.partial(share_kernel, later),
        [shape((SIDE * rows, own), bf16)] * len(later),
        [ynorm, out_weight],
        place,
        flops=2 * rows * width * len(later) * SIDE * own,
    )
    made = dict(zip(soon + later, [*early, *late]))
    shares = [made[k] for k in range(RING)]
    summed = reduce_ring(shares)
    return tokens.astype(f32) + summed[:rows] + to_side(summed[rows:].astype(bf16)).astype(f32)


def solution(mesh):
    return jax.shard_map(
        local,
        mesh=mesh,
        in_specs=(
            P("section", "head"),
            P(),
            P(None, "head"),
            P(None, "head"),
            P(None, "head"),
            P("head"),
            P("head"),
            P("head"),
            P("head", None),
            P("head"),
            P("head", None),
        ),
        out_specs=P("section", "head"),
        check_vma=False,
    )
```

```python
import functools

import jax
import jax.numpy as jnp
from jax import lax
from jax.experimental import pallas as pl
from jax.experimental.pallas import tpu as pltpu
from jax.sharding import PartitionSpec as P

eps = 1e-05
RING = 8
SIDE = 2
ROW = 8
HEADS = 16
f32 = jnp.float32
bf16 = jnp.bfloat16
VMEM_BYTES = 24 * 1024 * 1024


def dot(a, b, dims=((1,), (0,))):
    return lax.dot_general(a, b, (dims, ((), ())), preferred_element_type=f32)


def silu(v):
    return v / (1.0 + jnp.exp(-v))


def softplus(v):
    return jnp.maximum(v, 0.0) + jnp.log1p(jnp.exp(-jnp.abs(v)))


def iota(shape, dim):
    return lax.broadcasted_iota(jnp.int32, shape, dim)


def split(v):
    high = v.astype(bf16)
    return high, (v - high.astype(f32)).astype(bf16)


def dot_pair(a, exact, dims=((1,), (0,))):
    high, low = split(a)
    return dot(high, exact, dims) + dot(low, exact, dims)


def dot_three(a, b, dims=((1,), (0,))):
    a_high, a_low = split(a)
    b_high, b_low = split(b)
    return dot(a_high, b_high, dims) + (dot(a_high, b_low, dims) + dot(a_low, b_high, dims))


def running_sum(v):
    count = v.shape[1]
    upper = (iota((count, count), 0) <= iota((count, count), 1)).astype(bf16)
    high, middle = split(v)
    low = (v - high.astype(f32) - middle.astype(f32)).astype(bf16)
    return dot(high, upper) + (dot(middle, upper) + dot(low, upper))


def owners(width, size_p):
    return iota((HEADS, width), 1) // size_p == iota((HEADS, width), 0)


def spread(heads_on_lanes, width, size_p):
    return dot_pair(heads_on_lanes, owners(width, size_p).astype(bf16))


def spread_row(heads_on_rows, width, size_p):
    return jnp.sum(jnp.where(owners(width, size_p), heads_on_rows, 0.0), axis=0, keepdims=True)


def stood(row):
    square = iota((HEADS, HEADS), 0) == iota((HEADS, HEADS), 1)
    return jnp.sum(jnp.where(square, row, 0.0), axis=1, keepdims=True)


def log_rows(row):
    high = row.astype(bf16).astype(f32)
    low = row - high
    return jnp.concatenate([high, low, jnp.zeros((14, row.shape[1]), f32)], 0).astype(bf16)


def log_row(block):
    tail = block[block.shape[0] - 16 :].astype(f32)
    return tail[0:1] + tail[1:2]


def norm_kernel(rows, place, *refs):
    blocks = refs[:RING]
    small, normed, bc_half = refs[RING:]
    own = blocks[0].shape[1]
    side, turn = place[0], place[1]
    piece = blocks[0].shape[0] // SIDE

    def parts():
        for k in range(RING):
            for j in range(SIDE):
                head = lax.rem(side + j, SIDE) * RING + lax.rem(turn + k, RING)
                yield blocks[k], j * piece, head

    squares = jnp.zeros((rows, own), f32)
    for block, at, _ in parts():
        value = block[at : at + rows, :].astype(f32)
        squares = squares + value * value
    mean = jnp.sum(squares, axis=1, keepdims=True) / (RING * SIDE * own)
    scale = lax.rsqrt(mean + eps)
    for block, at, head in parts():
        value = block[at : at + rows, :].astype(f32)
        spot = pl.multiple_of(head * own, own)
        normed[:, pl.ds(spot, own)] = (value * scale * small[pl.ds(head + 8, 1), :]).astype(bf16)
        bc_half[pl.ds(spot, own), :] = block[at + rows : at + piece, :]


def project_kernel(heads, size_p, normed, x_weight, dt_weight, small, x_out, tailed_out, cums_out, step_out):
    rows = normed.shape[0]
    width = heads * size_p
    whole = normed[...]
    raw = dot(whole, dt_weight[...], ((1,), (1,))).T[0:HEADS, :]
    step = softplus(raw + stood(small[0:1, 0:HEADS]))
    decay = -stood(small[1:2, 0:HEADS]) * step
    cums = running_sum(decay)
    tail = (jnp.exp(cums[:, rows - 1 : rows] - cums) * step).T
    x = silu(dot(whole, x_weight[...]))
    x_out[...] = x
    tailed_out[...] = x * spread(tail, width, size_p)
    cums_out[...] = cums
    step_out[...] = step


def state_kernel(size_p, place, normed, tailed, bc_mine, bc_other, cums, both_out, slots):
    rows, width = tailed.shape
    state_n = bc_mine.shape[1]
    half = width // 2
    first = place[2] == 0
    one, two = dot(normed[...], bc_mine[...]), dot(normed[...], bc_other[...])
    writes, reads = jnp.where(first, one, two), jnp.where(first, two, one)
    both_out[:, 0:state_n] = writes
    both_out[:, state_n:] = reads
    state = dot_three(writes.T, tailed[...]).astype(bf16)
    logs = log_rows(spread_row(cums[:, rows - 1 : rows], width, size_p))
    for i in range(slots.shape[0]):
        at = i % 2 * half
        slots[i, 0:state_n, :] = state[:, at : at + half]
        slots[i, state_n : state_n + 16, :] = logs[:, at : at + half]


def row_kernel(place, gathered, copies, own_out, pair_out, logs_out):
    state_n, half = gathered.shape[1] - 16, gathered.shape[2]
    core, spot = place[2], place[3]
    pair = spot + 1 - 2 * core
    state = jnp.zeros((state_n, half), f32)
    log = jnp.zeros((1, half), f32)
    own, other, own_log, other_log = state, state, log, log
    for i in range(gathered.shape[0]):
        own, own_log = jnp.where(i == spot, state, own), jnp.where(i == spot, log, own_log)
        other, other_log = jnp.where(i == pair, state, other), jnp.where(i == pair, log, other_log)
        here = log_row(gathered[i])
        state = jnp.exp(here) * state + gathered[i, 0:state_n, :].astype(f32)
        log = log + here
    own_out[...] = own
    pair_out[...] = other
    logs_out[0:1, :] = own_log
    logs_out[1:2, :] = other_log
    value, logs = state.astype(bf16), log_rows(log)
    for i in range(copies.shape[0]):
        copies[i, 0:state_n, :] = value
        copies[i, state_n : state_n + 16, :] = logs


def prefix_kernel(place, gathered, own, pair, logs, keep, send):
    state_n = own.shape[0]
    row = place[4]
    state = jnp.zeros(own.shape, f32)
    for i in range(gathered.shape[0] - 1):
        passed = jnp.exp(log_row(gathered[i])) * state + gathered[i, 0:state_n, :].astype(f32)
        state = jnp.where(i < row, passed, state)
    keep[...] = (jnp.exp(logs[0:1, :]) * state + own[...]).astype(bf16)
    send[...] = (jnp.exp(logs[1:2, :]) * state + pair[...]).astype(bf16)


def scan_kernel(heads, size_p, block, normed, gate_weight, x_in, both_in, cums_in, step_in, small, result, opened):
    rows, width = x_in.shape
    state_n = both_in.shape[1] // 2
    opened[...] = silu(dot(normed[...], gate_weight[...]))
    lower = iota((block, block), 0) >= iota((block, block), 1)
    skip = spread_row(stood(small[2:3, 0:HEADS]), width, size_p)
    state = None
    base = None
    for b in range(rows // block):
        span = slice(b * block, (b + 1) * block)
        x, writes, reads = x_in[span, :], both_in[span, 0:state_n], both_in[span, state_n:]
        cums_t, step_t = cums_in[:, span], step_in[:, span]
        cums = cums_t.T
        scores = dot_three(reads, writes, ((1,), (1,)))
        made = []
        for h in range(heads):
            gap = cums[:, h : h + 1] - cums_t[h : h + 1, :]
            mixing = jnp.exp(jnp.where(lower, gap, -jnp.inf)) * scores * step_t[h : h + 1, :]
            made.append(dot(mixing.astype(bf16), x[:, h * size_p : (h + 1) * size_p].astype(bf16)))
        y = jnp.concatenate(made, axis=1) + skip * x
        if state is not None:
            y = y + spread(jnp.exp(cums_t - base).T, width, size_p) * dot_three(reads, state)
        result[span, :] = y
        if (b + 1) * block < rows:
            last = cums_t[:, block - 1 : block]
            tail = (jnp.exp(last - cums_t) * step_t).T
            fresh = dot_three(writes.T, x * spread(tail, width, size_p))
            if state is not None:
                fresh = jnp.exp(spread_row(last - base, width, size_p)) * state + fresh
            state, base = fresh, last


def share(ynorm, out_weight, place, k, out):
    rows, own = ynorm.shape[0], out.shape[1]
    for j in range(SIDE):
        head = lax.rem(place[0] + j, SIDE) * RING + lax.rem(place[1] + k, RING)
        spot = pl.multiple_of(head * own, own)
        out[j * rows : (j + 1) * rows, :] = dot(ynorm, out_weight[:, pl.ds(spot, own)]).astype(bf16)


def finish_kernel(size_p, ks, place, result, opened, both, cums, keep, other, out_gain, out_weight, ynorm_out, *shares):
    rows, width = result.shape
    state_n = both.shape[1] // 2
    first = place[2] == 0
    left, right = jnp.where(first, keep[...], other[...]), jnp.where(first, other[...], keep[...])
    state = jnp.concatenate([left, right], axis=1)
    carried = dot_pair(both[:, state_n:], state)
    y = result[...] + spread(jnp.exp(cums[...]).T, width, size_p) * carried
    g = y * opened[...]
    same = (iota((width, width), 0) // size_p == iota((width, width), 1) // size_p).astype(bf16)
    mean = dot_pair(g * g, same) / size_p
    ynorm = (g * lax.rsqrt(mean + eps) * out_gain[...]).astype(bf16)
    ynorm_out[...] = ynorm
    for k, out in zip(ks, shares):
        share(ynorm, out_weight, place, k, out)


def share_kernel(ks, place, ynorm, out_weight, *shares):
    for k, out in zip(ks, shares):
        share(ynorm[...], out_weight, place, k, out)


def on_chip(kernel, outs, args, place=None, scratch=(), flops=0, transcendentals=0):
    specs = [pl.BlockSpec(memory_space=pltpu.VMEM)] * len(args)
    if place is not None:
        specs = [pl.BlockSpec(memory_space=pltpu.SMEM)] + specs
        args = [place] + list(args)
    moved = sum(a.size * a.dtype.itemsize for a in list(args) + list(outs))
    return pl.pallas_call(
        kernel,
        out_shape=outs,
        in_specs=specs,
        out_specs=[pl.BlockSpec(memory_space=pltpu.VMEM)] * len(outs),
        scratch_shapes=scratch,
        cost_estimate=pl.CostEstimate(flops=flops, bytes_accessed=moved, transcendentals=transcendentals),
        compiler_params=pltpu.CompilerParams(vmem_limit_bytes=VMEM_BYTES),
    )(*args)


def shape(dims, kind=f32):
    return jax.ShapeDtypeStruct(dims, kind)


def to_turn(block, step):
    route = [(i, i // RING * RING + (i + step) % RING) for i in range(SIDE * RING)]
    return lax.ppermute(block, "head", route)


def to_side(block):
    return lax.ppermute(block, "head", [(i, (i + RING) % (SIDE * RING)) for i in range(SIDE * RING)])


def to_core(block):
    return lax.ppermute(block, "section", [(i, i ^ 1) for i in range(lax.axis_size("section"))])


def gather_ring(block):
    found = {0: block}
    for k in range(1, RING // 2):
        found[k] = to_turn(found[k - 1], -1)
        found[RING - k] = to_turn(found[(RING - k + 1) % RING], 1)
    found[RING // 2] = to_turn(found[RING // 2 - 1], -1)
    return [found[k] for k in range(RING)]


def add(a, b):
    return (a.astype(f32) + b.astype(f32)).astype(bf16)


def reduce_ring(shares):
    far = RING // 2
    up = to_turn(shares[far], 1)
    down = None
    for k in range(far - 1, 0, -1):
        back = shares[RING - k]
        up = to_turn(add(up, shares[k]), 1)
        down = to_turn(back if down is None else add(down, back), -1)
    return shares[0].astype(f32) + up.astype(f32) + down.astype(f32)


def local(
    tokens,
    norm_gain,
    x_weight,
    gate_weight,
    dt_weight,
    dt_bias,
    decay_rate,
    skip_gain,
    bc_weight,
    out_gain,
    out_weight,
):
    rows, own = tokens.shape
    heads = decay_rate.shape[0]
    width = x_weight.shape[1]
    size_p = width // heads
    state_n = bc_weight.shape[1] // 2
    groups = lax.axis_size("head")
    sections = lax.axis_size("section")
    model = groups * own
    half = width // 2
    head, section = lax.axis_index("head"), lax.axis_index("section")
    place = jnp.stack([head // RING, head % RING, section % 2, section % ROW, section // ROW]).astype(jnp.int32)

    piece = lax.dynamic_slice_in_dim(bc_weight, section % 2 * state_n, state_n, 1)
    packed = jnp.concatenate([tokens, piece], 0)
    far = RING // 2
    blocks = gather_ring(jnp.concatenate([packed, to_side(packed)], 0))
    dt_wide = jnp.pad(dt_weight.T, ((0, 128 - heads), (0, 0)))
    small = jnp.zeros((8 + groups, own), f32)
    small = small.at[0, :heads].set(dt_bias).at[1, :heads].set(decay_rate).at[2, :heads].set(skip_gain)
    small = small.at[8:].set(norm_gain.reshape(groups, own))
    normed, bc_mine = on_chip(
        functools.partial(norm_kernel, rows),
        [shape((rows, model), bf16), shape((model, state_n), bf16)],
        [*blocks, small],
        place,
    )
    bc_other = to_core(bc_mine)
    x, tailed, cums, step = on_chip(
        functools.partial(project_kernel, heads, size_p),
        [shape((rows, width)), shape((rows, width)), shape((HEADS, rows)), shape((HEADS, rows))],
        [normed, x_weight, dt_wide, small],
        flops=2 * rows * model * (width + 128),
    )
    both, slots = on_chip(
        functools.partial(state_kernel, size_p),
        [shape((rows, 2 * state_n)), shape((ROW, state_n + 16, half), bf16)],
        [normed, tailed, bc_mine, bc_other, cums],
        place,
        flops=2 * rows * model * 2 * state_n,
    )
    result, opened = on_chip(
        functools.partial(scan_kernel, heads, size_p, 256),
        [shape((rows, width)), shape((rows, width))],
        [normed, gate_weight, x, both, cums, step, small],
        flops=2 * rows * model * width + 12 * rows * 256 * (width + 3 * state_n),
        transcendentals=heads * rows * 256,
    )
    lines = sections // ROW
    by_row = [list(range(r * ROW, (r + 1) * ROW)) for r in range(lines)]
    by_spot = [list(range(p, sections, ROW)) for p in range(ROW)]
    copies, enter_own, enter_pair, logs = on_chip(
        row_kernel,
        [shape((lines, state_n + 16, half), bf16), shape((state_n, half)), shape((state_n, half)), shape((8, half))],
        [lax.all_to_all(slots, "section", 0, 0, axis_index_groups=by_row)],
        place,
    )
    keep, send = on_chip(
        prefix_kernel,
        [shape((state_n, half), bf16), shape((state_n, half), bf16)],
        [lax.all_to_all(copies, "section", 0, 0, axis_index_groups=by_spot), enter_own, enter_pair, logs],
        place,
    )
    rest = to_core(send)
    soon, later = (far, far + 1), tuple(k for k in range(RING) if k // 2 != RING // 4)
    ynorm, *early = on_chip(
        functools.partial(finish_kernel, size_p, soon),
        [shape((rows, width), bf16)] + [shape((SIDE * rows, own), bf16)] * len(soon),
        [result, opened, both, cums, keep, rest, out_gain.reshape(1, width), out_weight],
        place,
        flops=2 * rows * width * (2 * SIDE * own + 4 * width),
    )
    late = on_chip(
        functools.partial(share_kernel, later),
        [shape((SIDE * rows, own), bf16)] * len(later),
        [ynorm, out_weight],
        place,
        flops=2 * rows * width * len(later) * SIDE * own,
    )
    made = dict(zip(soon + later, [*early, *late]))
    shares = [made[k] for k in range(RING)]
    summed = reduce_ring(shares)
    return tokens.astype(f32) + summed[:rows] + to_side(summed[rows:].astype(bf16)).astype(f32)


def solution(mesh):
    return jax.shard_map(
        local,
        mesh=mesh,
        in_specs=(
            P("section", "head"),
            P(),
            P(None, "head"),
            P(None, "head"),
            P(None, "head"),
            P("head"),
            P("head"),
            P("head"),
            P("head", None),
            P("head"),
            P("head", None),
        ),
        out_specs=P("section", "head"),
        check_vma=False,
    )
```

```python
import functools

import jax
import jax.numpy as jnp
from jax import lax
from jax.experimental import pallas as pl
from jax.experimental.pallas import tpu as pltpu
from jax.sharding import PartitionSpec as P

eps = 1e-05
RING = 8
SIDE = 2
ROW = 8
HEADS = 16
f32 = jnp.float32
bf16 = jnp.bfloat16
VMEM_BYTES = 24 * 1024 * 1024


def dot(a, b, dims=((1,), (0,))):
    return lax.dot_general(a, b, (dims, ((), ())), preferred_element_type=f32)


def silu(v):
    return v / (1.0 + jnp.exp(-v))


def softplus(v):
    return jnp.maximum(v, 0.0) + jnp.log1p(jnp.exp(-jnp.abs(v)))


def iota(shape, dim):
    return lax.broadcasted_iota(jnp.int32, shape, dim)


def split(v):
    high = v.astype(bf16)
    return high, (v - high.astype(f32)).astype(bf16)


def dot_pair(a, exact, dims=((1,), (0,))):
    high, low = split(a)
    return dot(high, exact, dims) + dot(low, exact, dims)


def dot_three(a, b, dims=((1,), (0,))):
    a_high, a_low = split(a)
    b_high, b_low = split(b)
    return dot(a_high, b_high, dims) + (dot(a_high, b_low, dims) + dot(a_low, b_high, dims))


def running_sum(v):
    count = v.shape[1]
    upper = (iota((count, count), 0) <= iota((count, count), 1)).astype(bf16)
    high, middle = split(v)
    low = (v - high.astype(f32) - middle.astype(f32)).astype(bf16)
    return dot(high, upper) + (dot(middle, upper) + dot(low, upper))


def owners(width, size_p):
    return iota((HEADS, width), 1) // size_p == iota((HEADS, width), 0)


def spread(heads_on_lanes, width, size_p):
    return dot_pair(heads_on_lanes, owners(width, size_p).astype(bf16))


def spread_row(heads_on_rows, width, size_p):
    return jnp.sum(jnp.where(owners(width, size_p), heads_on_rows, 0.0), axis=0, keepdims=True)


def stood(row):
    square = iota((HEADS, HEADS), 0) == iota((HEADS, HEADS), 1)
    return jnp.sum(jnp.where(square, row, 0.0), axis=1, keepdims=True)


def log_rows(row):
    high = row.astype(bf16).astype(f32)
    low = row - high
    return jnp.concatenate([high, low, jnp.zeros((14, row.shape[1]), f32)], 0).astype(bf16)


def log_row(block):
    tail = block[block.shape[0] - 16 :].astype(f32)
    return tail[0:1] + tail[1:2]


def square_sum(rows, *blocks):
    value = jnp.zeros((rows, blocks[0].shape[1]), f32)
    for block in blocks:
        for j in range(SIDE):
            at = j * block.shape[0] // SIDE
            part = block[at : at + rows, :].astype(f32)
            value = value + part * part
    return value


def square_kernel(rows, *refs):
    refs[-1][...] = square_sum(rows, *refs[:-1])


def join_kernel(one, two, out):
    rows = one.shape[0]
    out[0:rows, :] = one[...]
    out[rows : 2 * rows, :] = two[...]


def norm_kernel(rows, place, *refs):
    blocks = refs[:RING]
    early, small, normed, bc_half = refs[RING:]
    own = blocks[0].shape[1]
    side, turn = place[0], place[1]
    piece = blocks[0].shape[0] // SIDE

    def parts():
        for k in range(RING):
            for j in range(SIDE):
                head = lax.rem(side + j, SIDE) * RING + lax.rem(turn + k, RING)
                yield blocks[k], j * piece, head

    squares = early[...] + square_sum(rows, blocks[RING // 2])
    mean = jnp.sum(squares, axis=1, keepdims=True) / (RING * SIDE * own)
    scale = lax.rsqrt(mean + eps)
    for block, at, head in parts():
        value = block[at : at + rows, :].astype(f32)
        spot = pl.multiple_of(head * own, own)
        normed[:, pl.ds(spot, own)] = (value * scale * small[pl.ds(head + 8, 1), :]).astype(bf16)
        bc_half[pl.ds(spot, own), :] = block[at + rows : at + piece, :]


def project_kernel(heads, size_p, normed, x_weight, dt_weight, small, x_out, tailed_out, cums_out, step_out):
    rows = normed.shape[0]
    width = heads * size_p
    whole = normed[...]
    raw = dot(whole, dt_weight[...], ((1,), (1,))).T[0:HEADS, :]
    step = softplus(raw + stood(small[0:1, 0:HEADS]))
    decay = -stood(small[1:2, 0:HEADS]) * step
    cums = running_sum(decay)
    tail = (jnp.exp(cums[:, rows - 1 : rows] - cums) * step).T
    x = silu(dot(whole, x_weight[...]))
    x_out[...] = x
    tailed_out[...] = x * spread(tail, width, size_p)
    cums_out[...] = cums
    step_out[...] = step


def state_kernel(size_p, place, normed, tailed, bc_mine, bc_other, cums, both_out, slots):
    rows, width = tailed.shape
    state_n = bc_mine.shape[1]
    half = width // 2
    first = place[2] == 0
    one, two = dot(normed[...], bc_mine[...]), dot(normed[...], bc_other[...])
    writes, reads = jnp.where(first, one, two), jnp.where(first, two, one)
    both_out[:, 0:state_n] = writes
    both_out[:, state_n:] = reads
    state = dot_three(writes.T, tailed[...]).astype(bf16)
    logs = log_rows(spread_row(cums[:, rows - 1 : rows], width, size_p))
    for i in range(slots.shape[0]):
        at = i % 2 * half
        slots[i, 0:state_n, :] = state[:, at : at + half]
        slots[i, state_n : state_n + 16, :] = logs[:, at : at + half]


def row_kernel(place, gathered, row_out, own_out, pair_out, logs_out):
    state_n, half = gathered.shape[1] - 16, gathered.shape[2]
    core, spot = place[2], place[3]
    pair = spot + 1 - 2 * core
    state = jnp.zeros((state_n, half), f32)
    log = jnp.zeros((1, half), f32)
    own, other, own_log, other_log = state, state, log, log
    for i in range(gathered.shape[0]):
        own, own_log = jnp.where(i == spot, state, own), jnp.where(i == spot, log, own_log)
        other, other_log = jnp.where(i == pair, state, other), jnp.where(i == pair, log, other_log)
        here = log_row(gathered[i])
        state = jnp.exp(here) * state + gathered[i, 0:state_n, :].astype(f32)
        log = log + here
    own_out[...] = own
    pair_out[...] = other
    logs_out[0:1, :] = own_log
    logs_out[1:2, :] = other_log
    row_out[0:state_n, :] = state.astype(bf16)
    row_out[state_n : state_n + 16, :] = log_rows(log)


def prefix_kernel(own, pair, logs, after, *refs):
    totals, (keep, send) = refs[:-2], refs[-2:]
    state_n = own.shape[0]
    state = jnp.zeros(own.shape, f32)
    for row in reversed(totals):
        state = jnp.exp(log_row(row[...])) * state + row[0:state_n, :].astype(f32)
    keep[...] = (jnp.exp(logs[0:1, :]) * state + own[...]).astype(bf16)
    send[...] = (jnp.exp(logs[1:2, :]) * state + pair[...]).astype(bf16)


def scan_kernel(heads, size_p, block, normed, gate_weight, x_in, both_in, cums_in, step_in, small, after, result, opened, done):
    rows, width = x_in.shape
    state_n = both_in.shape[1] // 2
    done[...] = jnp.zeros_like(done)
    opened[...] = silu(dot(normed[...], gate_weight[...]))
    lower = iota((block, block), 0) >= iota((block, block), 1)
    skip = spread_row(stood(small[2:3, 0:HEADS]), width, size_p)
    state = None
    base = None
    for b in range(rows // block):
        span = slice(b * block, (b + 1) * block)
        x, writes, reads = x_in[span, :], both_in[span, 0:state_n], both_in[span, state_n:]
        cums_t, step_t = cums_in[:, span], step_in[:, span]
        cums = cums_t.T
        scores = dot_three(reads, writes, ((1,), (1,)))
        made = []
        for h in range(heads):
            gap = cums[:, h : h + 1] - cums_t[h : h + 1, :]
            mixing = jnp.exp(jnp.where(lower, gap, -jnp.inf)) * scores * step_t[h : h + 1, :]
            made.append(dot(mixing.astype(bf16), x[:, h * size_p : (h + 1) * size_p].astype(bf16)))
        y = jnp.concatenate(made, axis=1) + skip * x
        if state is not None:
            y = y + spread(jnp.exp(cums_t - base).T, width, size_p) * dot_three(reads, state)
        result[span, :] = y
        if (b + 1) * block < rows:
            last = cums_t[:, block - 1 : block]
            tail = (jnp.exp(last - cums_t) * step_t).T
            fresh = dot_three(writes.T, x * spread(tail, width, size_p))
            if state is not None:
                fresh = jnp.exp(spread_row(last - base, width, size_p)) * state + fresh
            state, base = fresh, last


def share(ynorm, out_weight, place, k, out):
    rows, own = ynorm.shape[0], out.shape[1]
    for j in range(SIDE):
        head = lax.rem(place[0] + j, SIDE) * RING + lax.rem(place[1] + k, RING)
        spot = pl.multiple_of(head * own, own)
        out[j * rows : (j + 1) * rows, :] = dot(ynorm, out_weight[:, pl.ds(spot, own)]).astype(bf16)


def finish_kernel(size_p, ks, place, result, opened, both, cums, keep, other, out_gain, out_weight, ynorm_out, *shares):
    rows, width = result.shape
    state_n = both.shape[1] // 2
    first = place[2] == 0
    left, right = jnp.where(first, keep[...], other[...]), jnp.where(first, other[...], keep[...])
    state = jnp.concatenate([left, right], axis=1)
    carried = dot_pair(both[:, state_n:], state)
    y = result[...] + spread(jnp.exp(cums[...]).T, width, size_p) * carried
    g = y * opened[...]
    same = (iota((width, width), 0) // size_p == iota((width, width), 1) // size_p).astype(bf16)
    mean = dot_pair(g * g, same) / size_p
    ynorm = (g * lax.rsqrt(mean + eps) * out_gain[...]).astype(bf16)
    ynorm_out[...] = ynorm
    for k, out in zip(ks, shares):
        share(ynorm, out_weight, place, k, out)


def share_kernel(ks, place, ynorm, out_weight, *shares):
    for k, out in zip(ks, shares):
        share(ynorm[...], out_weight, place, k, out)


def on_chip(kernel, outs, args, place=None, scratch=(), flops=0, transcendentals=0):
    specs = [pl.BlockSpec(memory_space=pltpu.VMEM)] * len(args)
    if place is not None:
        specs = [pl.BlockSpec(memory_space=pltpu.SMEM)] + specs
        args = [place] + list(args)
    moved = sum(a.size * a.dtype.itemsize for a in list(args) + list(outs))
    return pl.pallas_call(
        kernel,
        out_shape=outs,
        in_specs=specs,
        out_specs=[pl.BlockSpec(memory_space=pltpu.VMEM)] * len(outs),
        scratch_shapes=scratch,
        cost_estimate=pl.CostEstimate(flops=flops, bytes_accessed=moved, transcendentals=transcendentals),
        compiler_params=pltpu.CompilerParams(vmem_limit_bytes=VMEM_BYTES),
    )(*args)


def shape(dims, kind=f32):
    return jax.ShapeDtypeStruct(dims, kind)


def to_turn(block, step):
    route = [(i, i // RING * RING + (i + step) % RING) for i in range(SIDE * RING)]
    return lax.ppermute(block, "head", route)


def to_side(block):
    return lax.ppermute(block, "head", [(i, (i + RING) % (SIDE * RING)) for i in range(SIDE * RING)])


def to_core(block):
    return lax.ppermute(block, "section", [(i, i ^ 1) for i in range(lax.axis_size("section"))])


def to_row(block, count):
    sections, ahead = lax.axis_size("section"), count * ROW
    return lax.ppermute(block, "section", [(i, i + ahead) for i in range(sections - ahead)])


def gather_ring(block):
    found = {0: block}
    for k in range(1, RING // 2):
        found[k] = to_turn(found[k - 1], -1)
        found[RING - k] = to_turn(found[(RING - k + 1) % RING], 1)
    found[RING // 2] = to_turn(found[RING // 2 - 1], -1)
    return [found[k] for k in range(RING)]


def add(a, b):
    return (a.astype(f32) + b.astype(f32)).astype(bf16)


def reduce_ring(shares):
    far = RING // 2
    up = to_turn(shares[far], 1)
    down = None
    for k in range(far - 1, 0, -1):
        back = shares[RING - k]
        up = to_turn(add(up, shares[k]), 1)
        down = to_turn(back if down is None else add(down, back), -1)
    return shares[0].astype(f32) + up.astype(f32) + down.astype(f32)


def local(
    tokens,
    norm_gain,
    x_weight,
    gate_weight,
    dt_weight,
    dt_bias,
    decay_rate,
    skip_gain,
    bc_weight,
    out_gain,
    out_weight,
):
    rows, own = tokens.shape
    heads = decay_rate.shape[0]
    width = x_weight.shape[1]
    size_p = width // heads
    state_n = bc_weight.shape[1] // 2
    groups = lax.axis_size("head")
    sections = lax.axis_size("section")
    model = groups * own
    half = width // 2
    head, section = lax.axis_index("head"), lax.axis_index("section")
    place = jnp.stack([head // RING, head % RING, section % 2, section % ROW, section // ROW]).astype(jnp.int32)

    piece = lax.dynamic_slice_in_dim(bc_weight, section % 2 * state_n, state_n, 1)
    packed = jnp.concatenate([tokens, piece], 0)
    far = RING // 2
    joined = on_chip(join_kernel, [shape((SIDE * (rows + own), own), bf16)], [packed, to_side(packed)])[0]
    blocks = gather_ring(joined)
    early = on_chip(
        functools.partial(square_kernel, rows),
        [shape((rows, own))],
        [blocks[k] for k in range(RING) if k != far],
    )[0]
    dt_wide = jnp.pad(dt_weight.T, ((0, 128 - heads), (0, 0)))
    small = jnp.zeros((8 + groups, own), f32)
    small = small.at[0, :heads].set(dt_bias).at[1, :heads].set(decay_rate).at[2, :heads].set(skip_gain)
    small = small.at[8:].set(norm_gain.reshape(groups, own))
    normed, bc_mine = on_chip(
        functools.partial(norm_kernel, rows),
        [shape((rows, model), bf16), shape((model, state_n), bf16)],
        [*blocks, early, small],
        place,
    )
    bc_other = to_core(bc_mine)
    x, tailed, cums, step = on_chip(
        functools.partial(project_kernel, heads, size_p),
        [shape((rows, width)), shape((rows, width)), shape((HEADS, rows)), shape((HEADS, rows))],
        [normed, x_weight, dt_wide, small],
        flops=2 * rows * model * (width + 128),
    )
    both, slots = on_chip(
        functools.partial(state_kernel, size_p),
        [shape((rows, 2 * state_n)), shape((ROW, state_n + 16, half), bf16)],
        [normed, tailed, bc_mine, bc_other, cums],
        place,
        flops=2 * rows * model * 2 * state_n,
    )
    lines = sections // ROW
    by_row = [list(range(r * ROW, (r + 1) * ROW)) for r in range(lines)]
    row_total, enter_own, enter_pair, logs = on_chip(
        row_kernel,
        [shape((state_n + 16, half), bf16), shape((state_n, half)), shape((state_n, half)), shape((8, half))],
        [lax.all_to_all(slots, "section", 0, 0, axis_index_groups=by_row)],
        place,
    )
    above = [to_row(row_total, k) for k in range(1, lines)]
    result, opened, done = on_chip(
        functools.partial(scan_kernel, heads, size_p, 256),
        [shape((rows, width)), shape((rows, width)), shape((8, 128))],
        [normed, gate_weight, x, both, cums, step, small, logs],
        flops=2 * rows * model * width + 12 * rows * 256 * (width + 3 * state_n),
        transcendentals=heads * rows * 256,
    )
    keep, send = on_chip(
        prefix_kernel,
        [shape((state_n, half), bf16), shape((state_n, half), bf16)],
        [enter_own, enter_pair, logs, done, *above],
    )
    rest = to_core(send)
    soon, later = (far, far + 1), tuple(k for k in range(RING) if k // 2 != RING // 4)
    ynorm, *early = on_chip(
        functools.partial(finish_kernel, size_p, soon),
        [shape((rows, width), bf16)] + [shape((SIDE * rows, own), bf16)] * len(soon),
        [result, opened, both, cums, keep, rest, out_gain.reshape(1, width), out_weight],
        place,
        flops=2 * rows * width * (2 * SIDE * own + 4 * width),
    )
    late = on_chip(
        functools.partial(share_kernel, later),
        [shape((SIDE * rows, own), bf16)] * len(later),
        [ynorm, out_weight],
        place,
        flops=2 * rows * width * len(later) * SIDE * own,
    )
    made = dict(zip(soon + later, [*early, *late]))
    shares = [made[k] for k in range(RING)]
    summed = reduce_ring(shares)
    return tokens.astype(f32) + summed[:rows] + to_side(summed[rows:].astype(bf16)).astype(f32)


def solution(mesh):
    return jax.shard_map(
        local,
        mesh=mesh,
        in_specs=(
            P("section", "head"),
            P(),
            P(None, "head"),
            P(None, "head"),
            P(None, "head"),
            P("head"),
            P("head"),
            P("head"),
            P("head", None),
            P("head"),
            P("head", None),
        ),
        out_specs=P("section", "head"),
        check_vma=False,
    )
```

```python
import functools

import jax
import jax.numpy as jnp
from jax import lax
from jax.experimental import pallas as pl
from jax.experimental.pallas import tpu as pltpu
from jax.sharding import PartitionSpec as P

eps = 1e-05
RING = 8
SIDE = 2
ROW = 8
HEADS = 16
f32 = jnp.float32
bf16 = jnp.bfloat16
VMEM_BYTES = 24 * 1024 * 1024


def dot(a, b, dims=((1,), (0,))):
    return lax.dot_general(a, b, (dims, ((), ())), preferred_element_type=f32)


def silu(v):
    return v / (1.0 + jnp.exp(-v))


def softplus(v):
    return jnp.maximum(v, 0.0) + jnp.log1p(jnp.exp(-jnp.abs(v)))


def iota(shape, dim):
    return lax.broadcasted_iota(jnp.int32, shape, dim)


def split(v):
    high = v.astype(bf16)
    return high, (v - high.astype(f32)).astype(bf16)


def dot_pair(a, exact, dims=((1,), (0,))):
    high, low = split(a)
    return dot(high, exact, dims) + dot(low, exact, dims)


def dot_three(a, b, dims=((1,), (0,))):
    a_high, a_low = split(a)
    b_high, b_low = split(b)
    return dot(a_high, b_high, dims) + (dot(a_high, b_low, dims) + dot(a_low, b_high, dims))


def running_sum(v):
    count = v.shape[1]
    upper = (iota((count, count), 0) <= iota((count, count), 1)).astype(bf16)
    high, middle = split(v)
    low = (v - high.astype(f32) - middle.astype(f32)).astype(bf16)
    return dot(high, upper) + (dot(middle, upper) + dot(low, upper))


def owners(width, size_p):
    return iota((HEADS, width), 1) // size_p == iota((HEADS, width), 0)


def spread(heads_on_lanes, width, size_p):
    return dot_pair(heads_on_lanes, owners(width, size_p).astype(bf16))


def spread_row(heads_on_rows, width, size_p):
    return jnp.sum(jnp.where(owners(width, size_p), heads_on_rows, 0.0), axis=0, keepdims=True)


def stood(row):
    square = iota((HEADS, HEADS), 0) == iota((HEADS, HEADS), 1)
    return jnp.sum(jnp.where(square, row, 0.0), axis=1, keepdims=True)


def log_rows(row):
    high = row.astype(bf16).astype(f32)
    low = row - high
    return jnp.concatenate([high, low, jnp.zeros((14, row.shape[1]), f32)], 0).astype(bf16)


def log_row(block):
    tail = block[block.shape[0] - 16 :].astype(f32)
    return tail[0:1] + tail[1:2]


def distant(turn, k):
    return lax.rem(turn + jnp.where(lax.rem(turn, 2) == 0, k, RING - k), RING)


def square_sum(rows, *blocks):
    value = jnp.zeros((rows, blocks[0].shape[1]), f32)
    for block in blocks:
        for j in range(SIDE):
            at = j * block.shape[0] // SIDE
            part = block[at : at + rows, :].astype(f32)
            value = value + part * part
    return value


def square_kernel(rows, *refs):
    refs[-1][...] = square_sum(rows, *refs[:-1])


def join_kernel(one, two, out):
    rows = one.shape[0]
    out[0:rows, :] = one[...]
    out[rows : 2 * rows, :] = two[...]


def norm_kernel(rows, place, *refs):
    blocks = refs[:RING]
    early, small, normed, bc_half = refs[RING:]
    own = blocks[0].shape[1]
    side, turn = place[0], place[1]
    piece = blocks[0].shape[0] // SIDE

    def parts():
        for k in range(RING):
            for j in range(SIDE):
                head = lax.rem(side + j, SIDE) * RING + distant(turn, k)
                yield blocks[k], j * piece, head

    squares = early[...] + square_sum(rows, blocks[RING // 2])
    mean = jnp.sum(squares, axis=1, keepdims=True) / (RING * SIDE * own)
    scale = lax.rsqrt(mean + eps)
    for block, at, head in parts():
        value = block[at : at + rows, :].astype(f32)
        spot = pl.multiple_of(head * own, own)
        normed[:, pl.ds(spot, own)] = (value * scale * small[pl.ds(head + 8, 1), :]).astype(bf16)
        bc_half[pl.ds(spot, own), :] = block[at + rows : at + piece, :]


def project_kernel(heads, size_p, normed, x_weight, dt_weight, small, x_out, tailed_out, cums_out, step_out):
    rows = normed.shape[0]
    width = heads * size_p
    whole = normed[...]
    raw = dot(whole, dt_weight[...], ((1,), (1,))).T[0:HEADS, :]
    step = softplus(raw + stood(small[0:1, 0:HEADS]))
    decay = -stood(small[1:2, 0:HEADS]) * step
    cums = running_sum(decay)
    tail = (jnp.exp(cums[:, rows - 1 : rows] - cums) * step).T
    x = silu(dot(whole, x_weight[...]))
    x_out[...] = x
    tailed_out[...] = x * spread(tail, width, size_p)
    cums_out[...] = cums
    step_out[...] = step


def state_kernel(size_p, place, normed, tailed, bc_mine, bc_other, cums, both_out, slots):
    rows, width = tailed.shape
    state_n = bc_mine.shape[1]
    half = width // 2
    first = place[2] == 0
    one, two = dot(normed[...], bc_mine[...]), dot(normed[...], bc_other[...])
    writes, reads = jnp.where(first, one, two), jnp.where(first, two, one)
    both_out[:, 0:state_n] = writes
    both_out[:, state_n:] = reads
    state = dot_three(writes.T, tailed[...]).astype(bf16)
    logs = log_rows(spread_row(cums[:, rows - 1 : rows], width, size_p))
    for i in range(slots.shape[0]):
        at = i % 2 * half
        slots[i, 0:state_n, :] = state[:, at : at + half]
        slots[i, state_n : state_n + 16, :] = logs[:, at : at + half]


def row_kernel(place, gathered, row_out, own_out, pair_out, logs_out):
    state_n, half = gathered.shape[1] - 16, gathered.shape[2]
    core, spot = place[2], place[3]
    pair = spot + 1 - 2 * core
    state = jnp.zeros((state_n, half), f32)
    log = jnp.zeros((1, half), f32)
    own, other, own_log, other_log = state, state, log, log
    for i in range(gathered.shape[0]):
        own, own_log = jnp.where(i == spot, state, own), jnp.where(i == spot, log, own_log)
        other, other_log = jnp.where(i == pair, state, other), jnp.where(i == pair, log, other_log)
        here = log_row(gathered[i])
        state = jnp.exp(here) * state + gathered[i, 0:state_n, :].astype(f32)
        log = log + here
    own_out[...] = own
    pair_out[...] = other
    logs_out[0:1, :] = own_log
    logs_out[1:2, :] = other_log
    row_out[0:state_n, :] = state.astype(bf16)
    row_out[state_n : state_n + 16, :] = log_rows(log)


def prefix_kernel(own, pair, logs, after, *refs):
    totals, (keep, send) = refs[:-2], refs[-2:]
    state_n = own.shape[0]
    state = jnp.zeros(own.shape, f32)
    for row in reversed(totals):
        state = jnp.exp(log_row(row[...])) * state + row[0:state_n, :].astype(f32)
    keep[...] = (jnp.exp(logs[0:1, :]) * state + own[...]).astype(bf16)
    send[...] = (jnp.exp(logs[1:2, :]) * state + pair[...]).astype(bf16)


def scan_kernel(heads, size_p, block, normed, gate_weight, x_in, both_in, cums_in, step_in, small, after, result, opened, done):
    rows, width = x_in.shape
    state_n = both_in.shape[1] // 2
    done[...] = jnp.zeros_like(done)
    opened[...] = silu(dot(normed[...], gate_weight[...]))
    lower = iota((block, block), 0) >= iota((block, block), 1)
    skip = spread_row(stood(small[2:3, 0:HEADS]), width, size_p)
    state = None
    base = None
    for b in range(rows // block):
        span = slice(b * block, (b + 1) * block)
        x, writes, reads = x_in[span, :], both_in[span, 0:state_n], both_in[span, state_n:]
        cums_t, step_t = cums_in[:, span], step_in[:, span]
        cums = cums_t.T
        scores = dot_three(reads, writes, ((1,), (1,)))
        made = []
        for h in range(heads):
            gap = cums[:, h : h + 1] - cums_t[h : h + 1, :]
            mixing = jnp.exp(jnp.where(lower, gap, -jnp.inf)) * scores * step_t[h : h + 1, :]
            made.append(dot(mixing.astype(bf16), x[:, h * size_p : (h + 1) * size_p].astype(bf16)))
        y = jnp.concatenate(made, axis=1) + skip * x
        if state is not None:
            y = y + spread(jnp.exp(cums_t - base).T, width, size_p) * dot_three(reads, state)
        result[span, :] = y
        if (b + 1) * block < rows:
            last = cums_t[:, block - 1 : block]
            tail = (jnp.exp(last - cums_t) * step_t).T
            fresh = dot_three(writes.T, x * spread(tail, width, size_p))
            if state is not None:
                fresh = jnp.exp(spread_row(last - base, width, size_p)) * state + fresh
            state, base = fresh, last


def share(ynorm, out_weight, place, k, out):
    rows, own = ynorm.shape[0], out.shape[1]
    for j in range(SIDE):
        head = lax.rem(place[0] + j, SIDE) * RING + distant(place[1], k)
        spot = pl.multiple_of(head * own, own)
        out[j * rows : (j + 1) * rows, :] = dot(ynorm, out_weight[:, pl.ds(spot, own)]).astype(bf16)


def finish_kernel(size_p, ks, place, result, opened, both, cums, keep, other, out_gain, out_weight, ynorm_out, *shares):
    rows, width = result.shape
    state_n = both.shape[1] // 2
    first = place[2] == 0
    left, right = jnp.where(first, keep[...], other[...]), jnp.where(first, other[...], keep[...])
    state = jnp.concatenate([left, right], axis=1)
    carried = dot_pair(both[:, state_n:], state)
    y = result[...] + spread(jnp.exp(cums[...]).T, width, size_p) * carried
    g = y * opened[...]
    same = (iota((width, width), 0) // size_p == iota((width, width), 1) // size_p).astype(bf16)
    mean = dot_pair(g * g, same) / size_p
    ynorm = (g * lax.rsqrt(mean + eps) * out_gain[...]).astype(bf16)
    ynorm_out[...] = ynorm
    for k, out in zip(ks, shares):
        share(ynorm, out_weight, place, k, out)


def share_kernel(ks, place, ynorm, out_weight, *shares):
    for k, out in zip(ks, shares):
        share(ynorm[...], out_weight, place, k, out)


def on_chip(kernel, outs, args, place=None, scratch=(), flops=0, transcendentals=0):
    specs = [pl.BlockSpec(memory_space=pltpu.VMEM)] * len(args)
    if place is not None:
        specs = [pl.BlockSpec(memory_space=pltpu.SMEM)] + specs
        args = [place] + list(args)
    moved = sum(a.size * a.dtype.itemsize for a in list(args) + list(outs))
    return pl.pallas_call(
        kernel,
        out_shape=outs,
        in_specs=specs,
        out_specs=[pl.BlockSpec(memory_space=pltpu.VMEM)] * len(outs),
        scratch_shapes=scratch,
        cost_estimate=pl.CostEstimate(flops=flops, bytes_accessed=moved, transcendentals=transcendentals),
        compiler_params=pltpu.CompilerParams(vmem_limit_bytes=VMEM_BYTES),
    )(*args)


def shape(dims, kind=f32):
    return jax.ShapeDtypeStruct(dims, kind)


def to_turn(block, step):
    route = [(i, i // RING * RING + (i + step) % RING) for i in range(SIDE * RING)]
    return lax.ppermute(block, "head", route)


def to_side(block):
    return lax.ppermute(block, "head", [(i, (i + RING) % (SIDE * RING)) for i in range(SIDE * RING)])


def to_core(block):
    return lax.ppermute(block, "section", [(i, i ^ 1) for i in range(lax.axis_size("section"))])


def to_row(block, count):
    sections, ahead = lax.axis_size("section"), count * ROW
    return lax.ppermute(block, "section", [(i, i + ahead) for i in range(sections - ahead)])


def swap_turn(block, odd):
    route = []
    for i in range(SIDE * RING):
        ahead = 1 if i % 2 == odd else -1
        route.append((i, i // RING * RING + (i + ahead) % RING))
    return lax.ppermute(block, "head", route)


def gather_ring(block):
    far = RING // 2
    found = {0: block}
    for k in range(1, far):
        found[k], found[RING - k] = swap_turn(found[(RING - k + 1) % RING], 0), swap_turn(found[k - 1], 1)
    found[far] = swap_turn(found[far + 1], 0)
    return [found[k] for k in range(RING)]


def total(first, *others):
    value = first.astype(f32)
    for other in others:
        value = value + other.astype(f32)
    return value


def reduce_ring(shares):
    far = RING // 2
    one = swap_turn(shares[far], 0)
    two = swap_turn(shares[far - 1], 0)
    for k in range(far - 1, 0, -1):
        odd = (far - k) % 2
        one = swap_turn(total(shares[RING - k if odd else k], one).astype(bf16), odd)
        if k > 1:
            two = swap_turn(total(shares[RING - k + 1 if odd else k - 1], two).astype(bf16), odd)
    return total(shares[0], one, two)


def local(
    tokens,
    norm_gain,
    x_weight,
    gate_weight,
    dt_weight,
    dt_bias,
    decay_rate,
    skip_gain,
    bc_weight,
    out_gain,
    out_weight,
):
    rows, own = tokens.shape
    heads = decay_rate.shape[0]
    width = x_weight.shape[1]
    size_p = width // heads
    state_n = bc_weight.shape[1] // 2
    groups = lax.axis_size("head")
    sections = lax.axis_size("section")
    model = groups * own
    half = width // 2
    head, section = lax.axis_index("head"), lax.axis_index("section")
    place = jnp.stack([head // RING, head % RING, section % 2, section % ROW, section // ROW]).astype(jnp.int32)

    piece = lax.dynamic_slice_in_dim(bc_weight, section % 2 * state_n, state_n, 1)
    packed = jnp.concatenate([tokens, piece], 0)
    far = RING // 2
    joined = on_chip(join_kernel, [shape((SIDE * (rows + own), own), bf16)], [packed, to_side(packed)])[0]
    blocks = gather_ring(joined)
    early = on_chip(
        functools.partial(square_kernel, rows),
        [shape((rows, own))],
        [blocks[k] for k in range(RING) if k != far],
    )[0]
    dt_wide = jnp.pad(dt_weight.T, ((0, 128 - heads), (0, 0)))
    small = jnp.zeros((8 + groups, own), f32)
    small = small.at[0, :heads].set(dt_bias).at[1, :heads].set(decay_rate).at[2, :heads].set(skip_gain)
    small = small.at[8:].set(norm_gain.reshape(groups, own))
    normed, bc_mine = on_chip(
        functools.partial(norm_kernel, rows),
        [shape((rows, model), bf16), shape((model, state_n), bf16)],
        [*blocks, early, small],
        place,
    )
    bc_other = to_core(bc_mine)
    x, tailed, cums, step = on_chip(
        functools.partial(project_kernel, heads, size_p),
        [shape((rows, width)), shape((rows, width)), shape((HEADS, rows)), shape((HEADS, rows))],
        [normed, x_weight, dt_wide, small],
        flops=2 * rows * model * (width + 128),
    )
    both, slots = on_chip(
        functools.partial(state_kernel, size_p),
        [shape((rows, 2 * state_n)), shape((ROW, state_n + 16, half), bf16)],
        [normed, tailed, bc_mine, bc_other, cums],
        place,
        flops=2 * rows * model * 2 * state_n,
    )
    lines = sections // ROW
    by_row = [list(range(r * ROW, (r + 1) * ROW)) for r in range(lines)]
    row_total, enter_own, enter_pair, logs = on_chip(
        row_kernel,
        [shape((state_n + 16, half), bf16), shape((state_n, half)), shape((state_n, half)), shape((8, half))],
        [lax.all_to_all(slots, "section", 0, 0, axis_index_groups=by_row)],
        place,
    )
    above = [to_row(row_total, k) for k in range(1, lines)]
    result, opened, done = on_chip(
        functools.partial(scan_kernel, heads, size_p, 256),
        [shape((rows, width)), shape((rows, width)), shape((8, 128))],
        [normed, gate_weight, x, both, cums, step, small, logs],
        flops=2 * rows * model * width + 12 * rows * 256 * (width + 3 * state_n),
        transcendentals=heads * rows * 256,
    )
    keep, send = on_chip(
        prefix_kernel,
        [shape((state_n, half), bf16), shape((state_n, half), bf16)],
        [enter_own, enter_pair, logs, done, *above],
    )
    rest = to_core(send)
    soon, later = (far, far + 1), tuple(k for k in range(RING) if k // 2 != RING // 4)
    ynorm, *early = on_chip(
        functools.partial(finish_kernel, size_p, soon),
        [shape((rows, width), bf16)] + [shape((SIDE * rows, own), bf16)] * len(soon),
        [result, opened, both, cums, keep, rest, out_gain.reshape(1, width), out_weight],
        place,
        flops=2 * rows * width * (2 * SIDE * own + 4 * width),
    )
    late = on_chip(
        functools.partial(share_kernel, later),
        [shape((SIDE * rows, own), bf16)] * len(later),
        [ynorm, out_weight],
        place,
        flops=2 * rows * width * len(later) * SIDE * own,
    )
    made = dict(zip(soon + later, [*early, *late]))
    shares = [made[k] for k in range(RING)]
    summed = reduce_ring(shares)
    return tokens.astype(f32) + summed[:rows] + to_side(summed[rows:].astype(bf16)).astype(f32)


def solution(mesh):
    return jax.shard_map(
        local,
        mesh=mesh,
        in_specs=(
            P("section", "head"),
            P(),
            P(None, "head"),
            P(None, "head"),
            P(None, "head"),
            P("head"),
            P("head"),
            P("head"),
            P("head", None),
            P("head"),
            P("head", None),
        ),
        out_specs=P("section", "head"),
        check_vma=False,
    )
```

```python
import functools

import jax
import jax.numpy as jnp
from jax import lax
from jax.experimental import pallas as pl
from jax.experimental.pallas import tpu as pltpu
from jax.sharding import PartitionSpec as P

eps = 1e-05
RING = 8
SIDE = 2
ROW = 8
HEADS = 16
f32 = jnp.float32
bf16 = jnp.bfloat16
VMEM_BYTES = 24 * 1024 * 1024


def dot(a, b, dims=((1,), (0,))):
    return lax.dot_general(a, b, (dims, ((), ())), preferred_element_type=f32)


def silu(v):
    return v / (1.0 + jnp.exp(-v))


def softplus(v):
    return jnp.maximum(v, 0.0) + jnp.log1p(jnp.exp(-jnp.abs(v)))


def iota(shape, dim):
    return lax.broadcasted_iota(jnp.int32, shape, dim)


def split(v):
    high = v.astype(bf16)
    return high, (v - high.astype(f32)).astype(bf16)


def dot_pair(a, exact, dims=((1,), (0,))):
    high, low = split(a)
    return dot(high, exact, dims) + dot(low, exact, dims)


def dot_three(a, b, dims=((1,), (0,))):
    a_high, a_low = split(a)
    b_high, b_low = split(b)
    return dot(a_high, b_high, dims) + (dot(a_high, b_low, dims) + dot(a_low, b_high, dims))


def running_sum(v):
    count = v.shape[1]
    upper = (iota((count, count), 0) <= iota((count, count), 1)).astype(bf16)
    high, middle = split(v)
    low = (v - high.astype(f32) - middle.astype(f32)).astype(bf16)
    return dot(high, upper) + (dot(middle, upper) + dot(low, upper))


def owners(width, size_p):
    return iota((HEADS, width), 1) // size_p == iota((HEADS, width), 0)


def spread(heads_on_lanes, width, size_p):
    return dot_pair(heads_on_lanes, owners(width, size_p).astype(bf16))


def spread_row(heads_on_rows, width, size_p):
    return jnp.sum(jnp.where(owners(width, size_p), heads_on_rows, 0.0), axis=0, keepdims=True)


def stood(row):
    square = iota((HEADS, HEADS), 0) == iota((HEADS, HEADS), 1)
    return jnp.sum(jnp.where(square, row, 0.0), axis=1, keepdims=True)


def log_rows(row):
    high = row.astype(bf16).astype(f32)
    low = row - high
    return jnp.concatenate([high, low, jnp.zeros((14, row.shape[1]), f32)], 0).astype(bf16)


def log_row(block):
    tail = block[block.shape[0] - 16 :].astype(f32)
    return tail[0:1] + tail[1:2]


def distant(turn, k):
    return lax.rem(turn + jnp.where(lax.rem(turn, 2) == 0, k, RING - k), RING)


def square_sum(rows, *blocks):
    value = jnp.zeros((rows, blocks[0].shape[1]), f32)
    for block in blocks:
        for j in range(SIDE):
            at = j * block.shape[0] // SIDE
            part = block[at : at + rows, :].astype(f32)
            value = value + part * part
    return value


def square_kernel(rows, *refs):
    refs[-1][...] = square_sum(rows, *refs[:-1])


def join_kernel(one, two, out):
    rows = one.shape[0]
    out[0:rows, :] = one[...]
    out[rows : 2 * rows, :] = two[...]


def norm_kernel(rows, place, *refs):
    blocks = refs[:RING]
    early, small, normed, bc_half = refs[RING:]
    own = blocks[0].shape[1]
    side, turn = place[0], place[1]
    piece = blocks[0].shape[0] // SIDE

    def parts():
        for k in range(RING):
            for j in range(SIDE):
                head = lax.rem(side + j, SIDE) * RING + distant(turn, k)
                yield blocks[k], j * piece, head

    squares = early[...] + square_sum(rows, blocks[RING // 2])
    mean = jnp.sum(squares, axis=1, keepdims=True) / (RING * SIDE * own)
    scale = lax.rsqrt(mean + eps)
    for block, at, head in parts():
        value = block[at : at + rows, :].astype(f32)
        spot = pl.multiple_of(head * own, own)
        normed[:, pl.ds(spot, own)] = (value * scale * small[pl.ds(head + 8, 1), :]).astype(bf16)
        bc_half[pl.ds(spot, own), :] = block[at + rows : at + piece, :]


def project_kernel(heads, size_p, normed, x_weight, dt_weight, small, x_out, tailed_out, cums_out, step_out):
    rows = normed.shape[0]
    width = heads * size_p
    whole = normed[...]
    raw = dot(whole, dt_weight[...], ((1,), (1,))).T[0:HEADS, :]
    step = softplus(raw + stood(small[0:1, 0:HEADS]))
    decay = -stood(small[1:2, 0:HEADS]) * step
    cums = running_sum(decay)
    tail = (jnp.exp(cums[:, rows - 1 : rows] - cums) * step).T
    x = silu(dot(whole, x_weight[...]))
    x_out[...] = x
    tailed_out[...] = x * spread(tail, width, size_p)
    cums_out[...] = cums
    step_out[...] = step


def state_kernel(size_p, place, normed, tailed, bc_mine, bc_other, cums, both_out, slots):
    rows, width = tailed.shape
    state_n = bc_mine.shape[1]
    half = width // 2
    first = place[2] == 0
    one, two = dot(normed[...], bc_mine[...]), dot(normed[...], bc_other[...])
    writes, reads = jnp.where(first, one, two), jnp.where(first, two, one)
    both_out[:, 0:state_n] = writes
    both_out[:, state_n:] = reads
    state = dot_three(writes.T, tailed[...]).astype(bf16)
    logs = log_rows(spread_row(cums[:, rows - 1 : rows], width, size_p))
    for i in range(slots.shape[0]):
        at = i % 2 * half
        slots[i, 0:state_n, :] = state[:, at : at + half]
        slots[i, state_n : state_n + 16, :] = logs[:, at : at + half]


def row_kernel(place, gathered, row_out, own_out, pair_out, logs_out):
    state_n, half = gathered.shape[1] - 16, gathered.shape[2]
    core, spot = place[2], place[3]
    pair = spot + 1 - 2 * core
    state = jnp.zeros((state_n, half), f32)
    log = jnp.zeros((1, half), f32)
    own, other, own_log, other_log = state, state, log, log
    for i in range(gathered.shape[0]):
        own, own_log = jnp.where(i == spot, state, own), jnp.where(i == spot, log, own_log)
        other, other_log = jnp.where(i == pair, state, other), jnp.where(i == pair, log, other_log)
        here = log_row(gathered[i])
        state = jnp.exp(here) * state + gathered[i, 0:state_n, :].astype(f32)
        log = log + here
    own_out[...] = own
    pair_out[...] = other
    logs_out[0:1, :] = own_log
    logs_out[1:2, :] = other_log
    row_out[0:state_n, :] = state.astype(bf16)
    row_out[state_n : state_n + 16, :] = log_rows(log)


def prefix_kernel(own, pair, logs, after, *refs):
    totals, (keep, send) = refs[:-2], refs[-2:]
    state_n = own.shape[0]
    state = jnp.zeros(own.shape, f32)
    for row in reversed(totals):
        state = jnp.exp(log_row(row[...])) * state + row[0:state_n, :].astype(f32)
    keep[...] = (jnp.exp(logs[0:1, :]) * state + own[...]).astype(bf16)
    send[...] = (jnp.exp(logs[1:2, :]) * state + pair[...]).astype(bf16)


def scan_kernel(heads, size_p, block, normed, gate_weight, x_in, both_in, cums_in, step_in, small, after, result, opened, done):
    rows, width = x_in.shape
    state_n = both_in.shape[1] // 2
    done[...] = jnp.zeros_like(done)
    opened[...] = silu(dot(normed[...], gate_weight[...]))
    lower = iota((block, block), 0) >= iota((block, block), 1)
    skip = spread_row(stood(small[2:3, 0:HEADS]), width, size_p)
    state = None
    base = None
    for b in range(rows // block):
        span = slice(b * block, (b + 1) * block)
        x, writes, reads = x_in[span, :], both_in[span, 0:state_n], both_in[span, state_n:]
        cums_t, step_t = cums_in[:, span], step_in[:, span]
        cums = cums_t.T
        scores = dot_three(reads, writes, ((1,), (1,)))
        made = []
        for h in range(heads):
            gap = cums[:, h : h + 1] - cums_t[h : h + 1, :]
            mixing = jnp.exp(jnp.where(lower, gap, -jnp.inf)) * scores * step_t[h : h + 1, :]
            made.append(dot(mixing.astype(bf16), x[:, h * size_p : (h + 1) * size_p].astype(bf16)))
        y = jnp.concatenate(made, axis=1) + skip * x
        if state is not None:
            y = y + spread(jnp.exp(cums_t - base).T, width, size_p) * dot_three(reads, state)
        result[span, :] = y
        if (b + 1) * block < rows:
            last = cums_t[:, block - 1 : block]
            tail = (jnp.exp(last - cums_t) * step_t).T
            fresh = dot_three(writes.T, x * spread(tail, width, size_p))
            if state is not None:
                fresh = jnp.exp(spread_row(last - base, width, size_p)) * state + fresh
            state, base = fresh, last


def share(ynorm, out_weight, place, k, out):
    rows, own = ynorm.shape[0], out.shape[1]
    for j in range(SIDE):
        head = lax.rem(place[0] + j, SIDE) * RING + distant(place[1], k)
        spot = pl.multiple_of(head * own, own)
        out[j * rows : (j + 1) * rows, :] = dot(ynorm, out_weight[:, pl.ds(spot, own)]).astype(bf16)


def finish_kernel(size_p, ks, place, result, opened, both, cums, keep, other, out_gain, out_weight, ynorm_out, *shares):
    rows, width = result.shape
    state_n = both.shape[1] // 2
    first = place[2] == 0
    left, right = jnp.where(first, keep[...], other[...]), jnp.where(first, other[...], keep[...])
    state = jnp.concatenate([left, right], axis=1)
    carried = dot_pair(both[:, state_n:], state)
    y = result[...] + spread(jnp.exp(cums[...]).T, width, size_p) * carried
    g = y * opened[...]
    same = (iota((width, width), 0) // size_p == iota((width, width), 1) // size_p).astype(bf16)
    mean = dot_pair(g * g, same) / size_p
    ynorm = (g * lax.rsqrt(mean + eps) * out_gain[...]).astype(bf16)
    ynorm_out[...] = ynorm
    for k, out in zip(ks, shares):
        share(ynorm, out_weight, place, k, out)


def share_kernel(ks, place, ynorm, out_weight, *shares):
    for k, out in zip(ks, shares):
        share(ynorm[...], out_weight, place, k, out)


def on_chip(kernel, outs, args, place=None, scratch=(), flops=0, transcendentals=0):
    specs = [pl.BlockSpec(memory_space=pltpu.VMEM)] * len(args)
    if place is not None:
        specs = [pl.BlockSpec(memory_space=pltpu.SMEM)] + specs
        args = [place] + list(args)
    moved = sum(a.size * a.dtype.itemsize for a in list(args) + list(outs))
    return pl.pallas_call(
        kernel,
        out_shape=outs,
        in_specs=specs,
        out_specs=[pl.BlockSpec(memory_space=pltpu.VMEM)] * len(outs),
        scratch_shapes=scratch,
        cost_estimate=pl.CostEstimate(flops=flops, bytes_accessed=moved, transcendentals=transcendentals),
        compiler_params=pltpu.CompilerParams(vmem_limit_bytes=VMEM_BYTES),
    )(*args)


def shape(dims, kind=f32):
    return jax.ShapeDtypeStruct(dims, kind)


def to_turn(block, step):
    route = [(i, i // RING * RING + (i + step) % RING) for i in range(SIDE * RING)]
    return lax.ppermute(block, "head", route)


def to_side(block):
    return lax.ppermute(block, "head", [(i, (i + RING) % (SIDE * RING)) for i in range(SIDE * RING)])


def to_core(block):
    return lax.ppermute(block, "section", [(i, i ^ 1) for i in range(lax.axis_size("section"))])


def to_row(block, count):
    sections, ahead = lax.axis_size("section"), count * ROW
    return lax.ppermute(block, "section", [(i, i + ahead) for i in range(sections - ahead)])


def swap_turn(block, odd):
    route = []
    for i in range(SIDE * RING):
        ahead = 1 if i % 2 == odd else -1
        route.append((i, i // RING * RING + (i + ahead) % RING))
    return lax.ppermute(block, "head", route)


def gather_ring(block):
    far = RING // 2
    found = {0: block}
    for k in range(1, far):
        found[k], found[RING - k] = swap_turn(found[(RING - k + 1) % RING], 0), swap_turn(found[k - 1], 1)
    found[far] = swap_turn(found[far + 1], 0)
    return [found[k] for k in range(RING)]


def total(first, *others):
    value = first.astype(f32)
    for other in others:
        value = value + other.astype(f32)
    return value


def reduce_ring(shares):
    far = RING // 2
    one = swap_turn(shares[far], 0)
    two = swap_turn(shares[far - 1], 0)
    for k in range(far - 1, 0, -1):
        odd = (far - k) % 2
        one = swap_turn(total(shares[RING - k if odd else k], one).astype(bf16), odd)
        if k > 1:
            two = swap_turn(total(shares[RING - k + 1 if odd else k - 1], two).astype(bf16), odd)
    return total(shares[0], one, two)


def local(
    tokens,
    norm_gain,
    x_weight,
    gate_weight,
    dt_weight,
    dt_bias,
    decay_rate,
    skip_gain,
    bc_weight,
    out_gain,
    out_weight,
):
    rows, own = tokens.shape
    heads = decay_rate.shape[0]
    width = x_weight.shape[1]
    size_p = width // heads
    state_n = bc_weight.shape[1] // 2
    groups = lax.axis_size("head")
    sections = lax.axis_size("section")
    model = groups * own
    half = width // 2
    head, section = lax.axis_index("head"), lax.axis_index("section")
    place = jnp.stack([head // RING, head % RING, section % 2, section % ROW, section // ROW]).astype(jnp.int32)

    piece = jnp.where(section % 2 == 0, bc_weight[:, :state_n], bc_weight[:, state_n:])
    packed = jnp.concatenate([tokens, piece], 0)
    far = RING // 2
    joined = on_chip(join_kernel, [shape((SIDE * (rows + own), own), bf16)], [packed, to_side(packed)])[0]
    blocks = gather_ring(joined)
    early = on_chip(
        functools.partial(square_kernel, rows),
        [shape((rows, own))],
        [blocks[k] for k in range(RING) if k != far],
    )[0]
    dt_wide = jnp.pad(dt_weight.T, ((0, 128 - heads), (0, 0)))
    small = jnp.zeros((8 + groups, own), f32)
    small = small.at[0, :heads].set(dt_bias).at[1, :heads].set(decay_rate).at[2, :heads].set(skip_gain)
    small = small.at[8:].set(norm_gain.reshape(groups, own))
    normed, bc_mine = on_chip(
        functools.partial(norm_kernel, rows),
        [shape((rows, model), bf16), shape((model, state_n), bf16)],
        [*blocks, early, small],
        place,
    )
    bc_other = to_core(bc_mine)
    x, tailed, cums, step = on_chip(
        functools.partial(project_kernel, heads, size_p),
        [shape((rows, width)), shape((rows, width)), shape((HEADS, rows)), shape((HEADS, rows))],
        [normed, x_weight, dt_wide, small],
        flops=2 * rows * model * (width + 128),
    )
    both, slots = on_chip(
        functools.partial(state_kernel, size_p),
        [shape((rows, 2 * state_n)), shape((ROW, state_n + 16, half), bf16)],
        [normed, tailed, bc_mine, bc_other, cums],
        place,
        flops=2 * rows * model * 2 * state_n,
    )
    lines = sections // ROW
    by_row = [list(range(r * ROW, (r + 1) * ROW)) for r in range(lines)]
    row_total, enter_own, enter_pair, logs = on_chip(
        row_kernel,
        [shape((state_n + 16, half), bf16), shape((state_n, half)), shape((state_n, half)), shape((8, half))],
        [lax.all_to_all(slots, "section", 0, 0, axis_index_groups=by_row)],
        place,
    )
    above = [to_row(row_total, k) for k in range(1, lines)]
    result, opened, done = on_chip(
        functools.partial(scan_kernel, heads, size_p, 256),
        [shape((rows, width)), shape((rows, width)), shape((8, 128))],
        [normed, gate_weight, x, both, cums, step, small, logs],
        flops=2 * rows * model * width + 12 * rows * 256 * (width + 3 * state_n),
        transcendentals=heads * rows * 256,
    )
    keep, send = on_chip(
        prefix_kernel,
        [shape((state_n, half), bf16), shape((state_n, half), bf16)],
        [enter_own, enter_pair, logs, done, *above],
    )
    rest = to_core(send)
    soon, later = (far, far + 1), tuple(k for k in range(RING) if k // 2 != RING // 4)
    ynorm, *early = on_chip(
        functools.partial(finish_kernel, size_p, soon),
        [shape((rows, width), bf16)] + [shape((SIDE * rows, own), bf16)] * len(soon),
        [result, opened, both, cums, keep, rest, out_gain.reshape(1, width), out_weight],
        place,
        flops=2 * rows * width * (2 * SIDE * own + 4 * width),
    )
    late = on_chip(
        functools.partial(share_kernel, later),
        [shape((SIDE * rows, own), bf16)] * len(later),
        [ynorm, out_weight],
        place,
        flops=2 * rows * width * len(later) * SIDE * own,
    )
    made = dict(zip(soon + later, [*early, *late]))
    shares = [made[k] for k in range(RING)]
    summed = reduce_ring(shares)
    return tokens.astype(f32) + summed[:rows] + to_side(summed[rows:].astype(bf16)).astype(f32)


def solution(mesh):
    return jax.shard_map(
        local,
        mesh=mesh,
        in_specs=(
            P("section", "head"),
            P(),
            P(None, "head"),
            P(None, "head"),
            P(None, "head"),
            P("head"),
            P("head"),
            P("head"),
            P("head", None),
            P("head"),
            P("head", None),
        ),
        out_specs=P("section", "head"),
        check_vma=False,
    )
```

```python
import functools

import jax
import jax.numpy as jnp
from jax import lax
from jax.experimental import pallas as pl
from jax.experimental.pallas import tpu as pltpu
from jax.sharding import PartitionSpec as P

eps = 1e-05
RING = 8
SIDE = 2
ROW = 8
HEADS = 16
f32 = jnp.float32
bf16 = jnp.bfloat16
VMEM_BYTES = 24 * 1024 * 1024


def dot(a, b, dims=((1,), (0,))):
    return lax.dot_general(a, b, (dims, ((), ())), preferred_element_type=f32)


def silu(v):
    return v / (1.0 + jnp.exp(-v))


def softplus(v):
    return jnp.maximum(v, 0.0) + jnp.log1p(jnp.exp(-jnp.abs(v)))


def iota(shape, dim):
    return lax.broadcasted_iota(jnp.int32, shape, dim)


def split(v):
    high = v.astype(bf16)
    return high, (v - high.astype(f32)).astype(bf16)


def dot_pair(a, exact, dims=((1,), (0,))):
    high, low = split(a)
    return dot(high, exact, dims) + dot(low, exact, dims)


def dot_three(a, b, dims=((1,), (0,))):
    a_high, a_low = split(a)
    b_high, b_low = split(b)
    return dot(a_high, b_high, dims) + (dot(a_high, b_low, dims) + dot(a_low, b_high, dims))


def running_sum(v):
    count = v.shape[1]
    upper = (iota((count, count), 0) <= iota((count, count), 1)).astype(bf16)
    high, middle = split(v)
    low = (v - high.astype(f32) - middle.astype(f32)).astype(bf16)
    return dot(high, upper) + (dot(middle, upper) + dot(low, upper))


def owners(width, size_p):
    return iota((HEADS, width), 1) // size_p == iota((HEADS, width), 0)


def spread(heads_on_lanes, width, size_p):
    return dot_pair(heads_on_lanes, owners(width, size_p).astype(bf16))


def spread_row(heads_on_rows, width, size_p):
    return jnp.sum(jnp.where(owners(width, size_p), heads_on_rows, 0.0), axis=0, keepdims=True)


def stood(row):
    square = iota((HEADS, HEADS), 0) == iota((HEADS, HEADS), 1)
    return jnp.sum(jnp.where(square, row, 0.0), axis=1, keepdims=True)


def log_rows(row):
    high = row.astype(bf16).astype(f32)
    low = row - high
    return jnp.concatenate([high, low, jnp.zeros((14, row.shape[1]), f32)], 0).astype(bf16)


def log_row(block):
    tail = block[block.shape[0] - 16 :].astype(f32)
    return tail[0:1] + tail[1:2]


def distant(turn, k):
    return lax.rem(turn + jnp.where(lax.rem(turn, 2) == 0, k, RING - k), RING)


def square_sum(rows, *blocks):
    value = jnp.zeros((rows, blocks[0].shape[1]), f32)
    for block in blocks:
        for j in range(SIDE):
            at = j * block.shape[0] // SIDE
            part = block[at : at + rows, :].astype(f32)
            value = value + part * part
    return value


def square_kernel(rows, *refs):
    refs[-1][...] = square_sum(rows, *refs[:-1])


def join_kernel(one, two, out):
    rows = one.shape[0]
    out[0:rows, :] = one[...]
    out[rows : 2 * rows, :] = two[...]


def norm_kernel(rows, place, *refs):
    blocks = refs[:RING]
    early, small, normed, bc_half = refs[RING:]
    own = blocks[0].shape[1]
    side, turn = place[0], place[1]
    piece = blocks[0].shape[0] // SIDE

    def parts():
        for k in range(RING):
            for j in range(SIDE):
                head = lax.rem(side + j, SIDE) * RING + distant(turn, k)
                yield blocks[k], j * piece, head

    squares = early[...] + square_sum(rows, blocks[RING // 2])
    mean = jnp.sum(squares, axis=1, keepdims=True) / (RING * SIDE * own)
    scale = lax.rsqrt(mean + eps)
    for block, at, head in parts():
        value = block[at : at + rows, :].astype(f32)
        spot = pl.multiple_of(head * own, own)
        normed[:, pl.ds(spot, own)] = (value * scale * small[pl.ds(head + 8, 1), :]).astype(bf16)
        bc_half[pl.ds(spot, own), :] = block[at + rows : at + piece, :]


def project_kernel(heads, size_p, normed, x_weight, dt_weight, small, x_out, tailed_out, cums_out, step_out):
    rows = normed.shape[0]
    width = heads * size_p
    whole = normed[...]
    raw = dot(whole, dt_weight[...], ((1,), (1,))).T[0:HEADS, :]
    step = softplus(raw + stood(small[0:1, 0:HEADS]))
    decay = -stood(small[1:2, 0:HEADS]) * step
    cums = running_sum(decay)
    tail = (jnp.exp(cums[:, rows - 1 : rows] - cums) * step).T
    x = silu(dot(whole, x_weight[...]))
    x_out[...] = x
    tailed_out[...] = x * spread(tail, width, size_p)
    cums_out[...] = cums
    step_out[...] = step


def state_kernel(size_p, place, normed, tailed, bc_mine, bc_other, cums, both_out, slots):
    rows, width = tailed.shape
    state_n = bc_mine.shape[1]
    half = width // 2
    first = place[2] == 0
    one, two = dot(normed[...], bc_mine[...]), dot(normed[...], bc_other[...])
    writes, reads = jnp.where(first, one, two), jnp.where(first, two, one)
    both_out[:, 0:state_n] = writes
    both_out[:, state_n:] = reads
    state = dot_three(writes.T, tailed[...]).astype(bf16)
    logs = log_rows(spread_row(cums[:, rows - 1 : rows], width, size_p))
    for i in range(slots.shape[0]):
        at = i % 2 * half
        slots[i, 0:state_n, :] = state[:, at : at + half]
        slots[i, state_n : state_n + 16, :] = logs[:, at : at + half]


def row_kernel(place, gathered, row_out, own_out, pair_out, logs_out):
    state_n, half = gathered.shape[1] - 16, gathered.shape[2]
    core, spot = place[2], place[3]
    pair = spot + 1 - 2 * core
    state = jnp.zeros((state_n, half), f32)
    log = jnp.zeros((1, half), f32)
    own, other, own_log, other_log = state, state, log, log
    for i in range(gathered.shape[0]):
        own, own_log = jnp.where(i == spot, state, own), jnp.where(i == spot, log, own_log)
        other, other_log = jnp.where(i == pair, state, other), jnp.where(i == pair, log, other_log)
        here = log_row(gathered[i])
        state = jnp.exp(here) * state + gathered[i, 0:state_n, :].astype(f32)
        log = log + here
    own_out[...] = own
    pair_out[...] = other
    logs_out[0:1, :] = own_log
    logs_out[1:2, :] = other_log
    row_out[0:state_n, :] = state.astype(bf16)
    row_out[state_n : state_n + 16, :] = log_rows(log)


def prefix_kernel(own, pair, logs, after, *refs):
    totals, (keep, send) = refs[:-2], refs[-2:]
    state_n = own.shape[0]
    state = jnp.zeros(own.shape, f32)
    for row in reversed(totals):
        state = jnp.exp(log_row(row[...])) * state + row[0:state_n, :].astype(f32)
    keep[...] = (jnp.exp(logs[0:1, :]) * state + own[...]).astype(bf16)
    send[...] = (jnp.exp(logs[1:2, :]) * state + pair[...]).astype(bf16)


def scan_kernel(heads, size_p, block, normed, gate_weight, x_in, both_in, cums_in, step_in, small, after, result, opened, done):
    rows, width = x_in.shape
    state_n = both_in.shape[1] // 2
    done[...] = jnp.zeros_like(done)
    opened[...] = silu(dot(normed[...], gate_weight[...]))
    lower = iota((block, block), 0) >= iota((block, block), 1)
    skip = spread_row(stood(small[2:3, 0:HEADS]), width, size_p)
    state = None
    base = None
    for b in range(rows // block):
        span = slice(b * block, (b + 1) * block)
        x, writes, reads = x_in[span, :], both_in[span, 0:state_n], both_in[span, state_n:]
        cums_t, step_t = cums_in[:, span], step_in[:, span]
        cums = cums_t.T
        scores = dot_three(reads, writes, ((1,), (1,)))
        made = []
        for h in range(heads):
            gap = cums[:, h : h + 1] - cums_t[h : h + 1, :]
            mixing = jnp.exp(jnp.where(lower, gap, -jnp.inf)) * scores * step_t[h : h + 1, :]
            made.append(dot(mixing.astype(bf16), x[:, h * size_p : (h + 1) * size_p].astype(bf16)))
        y = jnp.concatenate(made, axis=1) + skip * x
        if state is not None:
            y = y + spread(jnp.exp(cums_t - base).T, width, size_p) * dot_three(reads, state)
        result[span, :] = y
        if (b + 1) * block < rows:
            last = cums_t[:, block - 1 : block]
            tail = (jnp.exp(last - cums_t) * step_t).T
            fresh = dot_three(writes.T, x * spread(tail, width, size_p))
            if state is not None:
                fresh = jnp.exp(spread_row(last - base, width, size_p)) * state + fresh
            state, base = fresh, last


def share(ynorm, out_weight, place, k, out):
    rows, own = ynorm.shape[0], out.shape[1]
    for j in range(SIDE):
        head = lax.rem(place[0] + j, SIDE) * RING + distant(place[1], k)
        spot = pl.multiple_of(head * own, own)
        out[j * rows : (j + 1) * rows, :] = dot(ynorm, out_weight[:, pl.ds(spot, own)]).astype(bf16)


def finish_kernel(size_p, ks, place, result, opened, both, cums, keep, other, out_gain, out_weight, ynorm_out, *shares):
    rows, width = result.shape
    state_n = both.shape[1] // 2
    first = place[2] == 0
    left, right = jnp.where(first, keep[...], other[...]), jnp.where(first, other[...], keep[...])
    state = jnp.concatenate([left, right], axis=1)
    carried = dot_pair(both[:, state_n:], state)
    y = result[...] + spread(jnp.exp(cums[...]).T, width, size_p) * carried
    g = y * opened[...]
    same = (iota((width, width), 0) // size_p == iota((width, width), 1) // size_p).astype(bf16)
    mean = dot_pair(g * g, same) / size_p
    ynorm = (g * lax.rsqrt(mean + eps) * out_gain[...]).astype(bf16)
    ynorm_out[...] = ynorm
    for k, out in zip(ks, shares):
        share(ynorm, out_weight, place, k, out)


def share_kernel(ks, place, ynorm, out_weight, *shares):
    for k, out in zip(ks, shares):
        share(ynorm[...], out_weight, place, k, out)


def on_chip(kernel, outs, args, place=None, scratch=(), flops=0, transcendentals=0):
    specs = [pl.BlockSpec(memory_space=pltpu.VMEM)] * len(args)
    if place is not None:
        specs = [pl.BlockSpec(memory_space=pltpu.SMEM)] + specs
        args = [place] + list(args)
    moved = sum(a.size * a.dtype.itemsize for a in list(args) + list(outs))
    return pl.pallas_call(
        kernel,
        out_shape=outs,
        in_specs=specs,
        out_specs=[pl.BlockSpec(memory_space=pltpu.VMEM)] * len(outs),
        scratch_shapes=scratch,
        cost_estimate=pl.CostEstimate(flops=flops, bytes_accessed=moved, transcendentals=transcendentals),
        compiler_params=pltpu.CompilerParams(vmem_limit_bytes=VMEM_BYTES),
    )(*args)


def shape(dims, kind=f32):
    return jax.ShapeDtypeStruct(dims, kind)


def to_turn(block, step):
    route = [(i, i // RING * RING + (i + step) % RING) for i in range(SIDE * RING)]
    return lax.ppermute(block, "head", route)


def to_side(block):
    return lax.ppermute(block, "head", [(i, (i + RING) % (SIDE * RING)) for i in range(SIDE * RING)])


def to_core(block):
    return lax.ppermute(block, "section", [(i, i ^ 1) for i in range(lax.axis_size("section"))])


def to_row(block, count):
    sections, ahead = lax.axis_size("section"), count * ROW
    return lax.ppermute(block, "section", [(i, i + ahead) for i in range(sections - ahead)])


def swap_turn(block, odd):
    route = []
    for i in range(SIDE * RING):
        ahead = 1 if i % 2 == odd else -1
        route.append((i, i // RING * RING + (i + ahead) % RING))
    return lax.ppermute(block, "head", route)


def gather_ring(block):
    far = RING // 2
    found = {0: block}
    for k in range(1, far):
        found[k], found[RING - k] = swap_turn(found[(RING - k + 1) % RING], 0), swap_turn(found[k - 1], 1)
    found[far] = swap_turn(found[far + 1], 0)
    return [found[k] for k in range(RING)]


def total(first, *others):
    value = first.astype(f32)
    for other in others:
        value = value + other.astype(f32)
    return value


def reduce_ring(shares):
    far = RING // 2
    one = swap_turn(shares[far], 1)
    two = swap_turn(shares[far + 1], 1)
    for k in range(far - 1, 0, -1):
        odd = (far - k + 1) % 2
        one = swap_turn(total(shares[RING - k if odd else k], one).astype(bf16), odd)
        if k > 1:
            two = swap_turn(total(shares[RING - k + 1 if odd else k - 1], two).astype(bf16), odd)
    return total(shares[0], one, two)


def local(
    tokens,
    norm_gain,
    x_weight,
    gate_weight,
    dt_weight,
    dt_bias,
    decay_rate,
    skip_gain,
    bc_weight,
    out_gain,
    out_weight,
):
    rows, own = tokens.shape
    heads = decay_rate.shape[0]
    width = x_weight.shape[1]
    size_p = width // heads
    state_n = bc_weight.shape[1] // 2
    groups = lax.axis_size("head")
    sections = lax.axis_size("section")
    model = groups * own
    half = width // 2
    head, section = lax.axis_index("head"), lax.axis_index("section")
    place = jnp.stack([head // RING, head % RING, section % 2, section % ROW, section // ROW]).astype(jnp.int32)

    piece = lax.dynamic_slice_in_dim(bc_weight, section % 2 * state_n, state_n, 1)
    packed = jnp.concatenate([tokens, piece], 0)
    far = RING // 2
    joined = on_chip(join_kernel, [shape((SIDE * (rows + own), own), bf16)], [packed, to_side(packed)])[0]
    blocks = gather_ring(joined)
    early = on_chip(
        functools.partial(square_kernel, rows),
        [shape((rows, own))],
        [blocks[k] for k in range(RING) if k != far],
    )[0]
    dt_wide = jnp.pad(dt_weight.T, ((0, 128 - heads), (0, 0)))
    small = jnp.zeros((8 + groups, own), f32)
    small = small.at[0, :heads].set(dt_bias).at[1, :heads].set(decay_rate).at[2, :heads].set(skip_gain)
    small = small.at[8:].set(norm_gain.reshape(groups, own))
    normed, bc_mine = on_chip(
        functools.partial(norm_kernel, rows),
        [shape((rows, model), bf16), shape((model, state_n), bf16)],
        [*blocks, early, small],
        place,
    )
    bc_other = to_core(bc_mine)
    x, tailed, cums, step = on_chip(
        functools.partial(project_kernel, heads, size_p),
        [shape((rows, width)), shape((rows, width)), shape((HEADS, rows)), shape((HEADS, rows))],
        [normed, x_weight, dt_wide, small],
        flops=2 * rows * model * (width + 128),
    )
    both, slots = on_chip(
        functools.partial(state_kernel, size_p),
        [shape((rows, 2 * state_n)), shape((ROW, state_n + 16, half), bf16)],
        [normed, tailed, bc_mine, bc_other, cums],
        place,
        flops=2 * rows * model * 2 * state_n,
    )
    lines = sections // ROW
    by_row = [list(range(r * ROW, (r + 1) * ROW)) for r in range(lines)]
    row_total, enter_own, enter_pair, logs = on_chip(
        row_kernel,
        [shape((state_n + 16, half), bf16), shape((state_n, half)), shape((state_n, half)), shape((8, half))],
        [lax.all_to_all(slots, "section", 0, 0, axis_index_groups=by_row)],
        place,
    )
    above = [to_row(row_total, k) for k in range(1, lines)]
    result, opened, done = on_chip(
        functools.partial(scan_kernel, heads, size_p, 256),
        [shape((rows, width)), shape((rows, width)), shape((8, 128))],
        [normed, gate_weight, x, both, cums, step, small, logs],
        flops=2 * rows * model * width + 12 * rows * 256 * (width + 3 * state_n),
        transcendentals=heads * rows * 256,
    )
    keep, send = on_chip(
        prefix_kernel,
        [shape((state_n, half), bf16), shape((state_n, half), bf16)],
        [enter_own, enter_pair, logs, done, *above],
    )
    rest = to_core(send)
    soon, later = (far, far + 1), tuple(k for k in range(RING) if k // 2 != RING // 4)
    ynorm, *early = on_chip(
        functools.partial(finish_kernel, size_p, soon),
        [shape((rows, width), bf16)] + [shape((SIDE * rows, own), bf16)] * len(soon),
        [result, opened, both, cums, keep, rest, out_gain.reshape(1, width), out_weight],
        place,
        flops=2 * rows * width * (2 * SIDE * own + 4 * width),
    )
    late = on_chip(
        functools.partial(share_kernel, later),
        [shape((SIDE * rows, own), bf16)] * len(later),
        [ynorm, out_weight],
        place,
        flops=2 * rows * width * len(later) * SIDE * own,
    )
    made = dict(zip(soon + later, [*early, *late]))
    shares = [made[k] for k in range(RING)]
    summed = reduce_ring(shares)
    return tokens.astype(f32) + summed[:rows] + to_side(summed[rows:].astype(bf16)).astype(f32)


def solution(mesh):
    return jax.shard_map(
        local,
        mesh=mesh,
        in_specs=(
            P("section", "head"),
            P(),
            P(None, "head"),
            P(None, "head"),
            P(None, "head"),
            P("head"),
            P("head"),
            P("head"),
            P("head", None),
            P("head"),
            P("head", None),
        ),
        out_specs=P("section", "head"),
        check_vma=False,
    )
```

```python
import functools

import jax
import jax.numpy as jnp
from jax import lax
from jax.experimental import pallas as pl
from jax.experimental.pallas import tpu as pltpu
from jax.sharding import PartitionSpec as P

eps = 1e-05
RING = 8
SIDE = 2
ROW = 8
HEADS = 16
f32 = jnp.float32
bf16 = jnp.bfloat16
VMEM_BYTES = 24 * 1024 * 1024


def dot(a, b, dims=((1,), (0,))):
    return lax.dot_general(a, b, (dims, ((), ())), preferred_element_type=f32)


def silu(v):
    return v / (1.0 + jnp.exp(-v))


def softplus(v):
    return jnp.maximum(v, 0.0) + jnp.log1p(jnp.exp(-jnp.abs(v)))


def iota(shape, dim):
    return lax.broadcasted_iota(jnp.int32, shape, dim)


def split(v):
    high = v.astype(bf16)
    return high, (v - high.astype(f32)).astype(bf16)


def dot_pair(a, exact, dims=((1,), (0,))):
    high, low = split(a)
    return dot(high, exact, dims) + dot(low, exact, dims)


def dot_three(a, b, dims=((1,), (0,))):
    a_high, a_low = split(a)
    b_high, b_low = split(b)
    return dot(a_high, b_high, dims) + (dot(a_high, b_low, dims) + dot(a_low, b_high, dims))


def running_sum(v):
    count = v.shape[1]
    upper = (iota((count, count), 0) <= iota((count, count), 1)).astype(bf16)
    high, middle = split(v)
    low = (v - high.astype(f32) - middle.astype(f32)).astype(bf16)
    return dot(high, upper) + (dot(middle, upper) + dot(low, upper))


def owners(width, size_p):
    return iota((HEADS, width), 1) // size_p == iota((HEADS, width), 0)


def spread(heads_on_lanes, width, size_p):
    return dot_pair(heads_on_lanes, owners(width, size_p).astype(bf16))


def spread_row(heads_on_rows, width, size_p):
    return jnp.sum(jnp.where(owners(width, size_p), heads_on_rows, 0.0), axis=0, keepdims=True)


def stood(row):
    square = iota((HEADS, HEADS), 0) == iota((HEADS, HEADS), 1)
    return jnp.sum(jnp.where(square, row, 0.0), axis=1, keepdims=True)


def log_rows(row):
    high = row.astype(bf16).astype(f32)
    low = row - high
    return jnp.concatenate([high, low, jnp.zeros((14, row.shape[1]), f32)], 0).astype(bf16)


def log_row(block):
    tail = block[block.shape[0] - 16 :].astype(f32)
    return tail[0:1] + tail[1:2]


def distant(turn, k):
    return lax.rem(turn + jnp.where(lax.rem(turn, 2) == 0, k, RING - k), RING)


def square_sum(rows, *blocks):
    value = jnp.zeros((rows, blocks[0].shape[1]), f32)
    for block in blocks:
        for j in range(SIDE):
            at = j * block.shape[0] // SIDE
            part = block[at : at + rows, :].astype(f32)
            value = value + part * part
    return value


def square_kernel(rows, *refs):
    refs[-1][...] = square_sum(rows, *refs[:-1])


def join_kernel(one, two, out):
    rows = one.shape[0]
    out[0:rows, :] = one[...]
    out[rows : 2 * rows, :] = two[...]


def norm_kernel(rows, place, *refs):
    blocks = refs[:RING]
    early, small, normed, bc_half = refs[RING:]
    own = blocks[0].shape[1]
    side, turn = place[0], place[1]
    piece = blocks[0].shape[0] // SIDE

    def parts():
        for k in range(RING):
            for j in range(SIDE):
                head = lax.rem(side + j, SIDE) * RING + distant(turn, k)
                yield blocks[k], j * piece, head

    squares = early[...] + square_sum(rows, blocks[RING // 2])
    mean = jnp.sum(squares, axis=1, keepdims=True) / (RING * SIDE * own)
    scale = lax.rsqrt(mean + eps)
    for block, at, head in parts():
        value = block[at : at + rows, :].astype(f32)
        spot = pl.multiple_of(head * own, own)
        normed[:, pl.ds(spot, own)] = (value * scale * small[pl.ds(head + 8, 1), :]).astype(bf16)
        bc_half[pl.ds(spot, own), :] = block[at + rows : at + piece, :]


def project_kernel(heads, size_p, normed, x_weight, dt_weight, small, x_out, tailed_out, cums_out, step_out):
    rows = normed.shape[0]
    width = heads * size_p
    whole = normed[...]
    raw = dot(whole, dt_weight[...], ((1,), (1,))).T[0:HEADS, :]
    step = softplus(raw + stood(small[0:1, 0:HEADS]))
    decay = -stood(small[1:2, 0:HEADS]) * step
    cums = running_sum(decay)
    tail = (jnp.exp(cums[:, rows - 1 : rows] - cums) * step).T
    x = silu(dot(whole, x_weight[...]))
    x_out[...] = x
    tailed_out[...] = x * spread(tail, width, size_p)
    cums_out[...] = cums
    step_out[...] = step


def state_kernel(size_p, place, normed, tailed, bc_mine, bc_other, cums, both_out, slots):
    rows, width = tailed.shape
    state_n = bc_mine.shape[1]
    half = width // 2
    first = place[2] == 0
    one, two = dot(normed[...], bc_mine[...]), dot(normed[...], bc_other[...])
    writes, reads = jnp.where(first, one, two), jnp.where(first, two, one)
    both_out[:, 0:state_n] = writes
    both_out[:, state_n:] = reads
    state = dot_three(writes.T, tailed[...]).astype(bf16)
    logs = log_rows(spread_row(cums[:, rows - 1 : rows], width, size_p))
    for i in range(slots.shape[0]):
        at = i % 2 * half
        slots[i, 0:state_n, :] = state[:, at : at + half]
        slots[i, state_n : state_n + 16, :] = logs[:, at : at + half]


def row_kernel(place, gathered, row_out, own_out, pair_out, logs_out):
    state_n, half = gathered.shape[1] - 16, gathered.shape[2]
    core, spot = place[2], place[3]
    pair = spot + 1 - 2 * core
    state = jnp.zeros((state_n, half), f32)
    log = jnp.zeros((1, half), f32)
    own, other, own_log, other_log = state, state, log, log
    for i in range(gathered.shape[0]):
        own, own_log = jnp.where(i == spot, state, own), jnp.where(i == spot, log, own_log)
        other, other_log = jnp.where(i == pair, state, other), jnp.where(i == pair, log, other_log)
        here = log_row(gathered[i])
        state = jnp.exp(here) * state + gathered[i, 0:state_n, :].astype(f32)
        log = log + here
    own_out[...] = own
    pair_out[...] = other
    logs_out[0:1, :] = own_log
    logs_out[1:2, :] = other_log
    row_out[0:state_n, :] = state.astype(bf16)
    row_out[state_n : state_n + 16, :] = log_rows(log)


def prefix_kernel(own, pair, logs, after, *refs):
    totals, (keep, send) = refs[:-2], refs[-2:]
    state_n = own.shape[0]
    state = jnp.zeros(own.shape, f32)
    for row in reversed(totals):
        state = jnp.exp(log_row(row[...])) * state + row[0:state_n, :].astype(f32)
    keep[...] = (jnp.exp(logs[0:1, :]) * state + own[...]).astype(bf16)
    send[...] = (jnp.exp(logs[1:2, :]) * state + pair[...]).astype(bf16)


def scan_kernel(heads, size_p, block, normed, gate_weight, x_in, both_in, cums_in, step_in, small, after, result, opened, done):
    rows, width = x_in.shape
    state_n = both_in.shape[1] // 2
    done[...] = jnp.zeros_like(done)
    opened[...] = silu(dot(normed[...], gate_weight[...]))
    lower = iota((block, block), 0) >= iota((block, block), 1)
    skip = spread_row(stood(small[2:3, 0:HEADS]), width, size_p)
    state = None
    base = None
    for b in range(rows // block):
        span = slice(b * block, (b + 1) * block)
        x, writes, reads = x_in[span, :], both_in[span, 0:state_n], both_in[span, state_n:]
        cums_t, step_t = cums_in[:, span], step_in[:, span]
        cums = cums_t.T
        scores = dot_three(reads, writes, ((1,), (1,)))
        made = []
        for h in range(heads):
            gap = cums[:, h : h + 1] - cums_t[h : h + 1, :]
            mixing = jnp.exp(jnp.where(lower, gap, -jnp.inf)) * scores * step_t[h : h + 1, :]
            made.append(dot(mixing.astype(bf16), x[:, h * size_p : (h + 1) * size_p].astype(bf16)))
        y = jnp.concatenate(made, axis=1) + skip * x
        if state is not None:
            y = y + spread(jnp.exp(cums_t - base).T, width, size_p) * dot_three(reads, state)
        result[span, :] = y
        if (b + 1) * block < rows:
            last = cums_t[:, block - 1 : block]
            tail = (jnp.exp(last - cums_t) * step_t).T
            fresh = dot_three(writes.T, x * spread(tail, width, size_p))
            if state is not None:
                fresh = jnp.exp(spread_row(last - base, width, size_p)) * state + fresh
            state, base = fresh, last


def share(ynorm, out_weight, place, k, out):
    rows, own = ynorm.shape[0], out.shape[1]
    for j in range(SIDE):
        head = lax.rem(place[0] + j, SIDE) * RING + distant(place[1], k)
        spot = pl.multiple_of(head * own, own)
        out[j * rows : (j + 1) * rows, :] = dot(ynorm, out_weight[:, pl.ds(spot, own)]).astype(bf16)


def finish_kernel(size_p, ks, place, result, opened, both, cums, keep, other, out_gain, out_weight, ynorm_out, *shares):
    rows, width = result.shape
    state_n = both.shape[1] // 2
    first = place[2] == 0
    left, right = jnp.where(first, keep[...], other[...]), jnp.where(first, other[...], keep[...])
    state = jnp.concatenate([left, right], axis=1)
    carried = dot_pair(both[:, state_n:], state)
    y = result[...] + spread(jnp.exp(cums[...]).T, width, size_p) * carried
    g = y * opened[...]
    same = (iota((width, width), 0) // size_p == iota((width, width), 1) // size_p).astype(bf16)
    mean = dot_pair(g * g, same) / size_p
    ynorm = (g * lax.rsqrt(mean + eps) * out_gain[...]).astype(bf16)
    ynorm_out[...] = ynorm
    for k, out in zip(ks, shares):
        share(ynorm, out_weight, place, k, out)


def share_kernel(ks, place, ynorm, out_weight, *shares):
    for k, out in zip(ks, shares):
        share(ynorm[...], out_weight, place, k, out)


def on_chip(kernel, outs, args, place=None, scratch=(), flops=0, transcendentals=0):
    specs = [pl.BlockSpec(memory_space=pltpu.VMEM)] * len(args)
    if place is not None:
        specs = [pl.BlockSpec(memory_space=pltpu.SMEM)] + specs
        args = [place] + list(args)
    moved = sum(a.size * a.dtype.itemsize for a in list(args) + list(outs))
    return pl.pallas_call(
        kernel,
        out_shape=outs,
        in_specs=specs,
        out_specs=[pl.BlockSpec(memory_space=pltpu.VMEM)] * len(outs),
        scratch_shapes=scratch,
        cost_estimate=pl.CostEstimate(flops=flops, bytes_accessed=moved, transcendentals=transcendentals),
        compiler_params=pltpu.CompilerParams(vmem_limit_bytes=VMEM_BYTES),
    )(*args)


def shape(dims, kind=f32):
    return jax.ShapeDtypeStruct(dims, kind)


def to_turn(block, step):
    route = [(i, i // RING * RING + (i + step) % RING) for i in range(SIDE * RING)]
    return lax.ppermute(block, "head", route)


def to_side(block):
    return lax.ppermute(block, "head", [(i, (i + RING) % (SIDE * RING)) for i in range(SIDE * RING)])


def to_core(block):
    return lax.ppermute(block, "section", [(i, i ^ 1) for i in range(lax.axis_size("section"))])


def to_row(block, count):
    sections, ahead = lax.axis_size("section"), count * ROW
    return lax.ppermute(block, "section", [(i, i + ahead) for i in range(sections - ahead)])


def swap_turn(block, odd):
    route = []
    for i in range(SIDE * RING):
        ahead = 1 if i % 2 == odd else -1
        route.append((i, i // RING * RING + (i + ahead) % RING))
    return lax.ppermute(block, "head", route)


def gather_ring(block):
    far = RING // 2
    found = {0: block}
    for k in range(1, far):
        found[k], found[RING - k] = swap_turn(found[(RING - k + 1) % RING], 0), swap_turn(found[k - 1], 1)
    found[far] = swap_turn(found[far + 1], 0)
    return [found[k] for k in range(RING)]


def total(first, *others):
    value = first.astype(f32)
    for other in others:
        value = value + other.astype(f32)
    return value


def reduce_ring(shares):
    far = RING // 2
    one = swap_turn(shares[far], 0)
    two = swap_turn(shares[far - 1], 0)
    for k in range(far - 1, 0, -1):
        odd = (far - k) % 2
        one = swap_turn(total(shares[RING - k if odd else k], one).astype(bf16), odd)
        if k > 1:
            two = swap_turn(total(shares[RING - k + 1 if odd else k - 1], two).astype(bf16), odd)
    return total(shares[0], one, two)


def local(
    tokens,
    norm_gain,
    x_weight,
    gate_weight,
    dt_weight,
    dt_bias,
    decay_rate,
    skip_gain,
    bc_weight,
    out_gain,
    out_weight,
):
    rows, own = tokens.shape
    heads = decay_rate.shape[0]
    width = x_weight.shape[1]
    size_p = width // heads
    state_n = bc_weight.shape[1] // 2
    groups = lax.axis_size("head")
    sections = lax.axis_size("section")
    model = groups * own
    half = width // 2
    head, section = lax.axis_index("head"), lax.axis_index("section")
    place = jnp.stack([head // RING, head % RING, section % 2, section % ROW, section // ROW]).astype(jnp.int32)

    piece = lax.dynamic_slice_in_dim(bc_weight, section % 2 * state_n, state_n, 1)
    packed = jnp.concatenate([tokens, piece], 0)
    far = RING // 2
    joined = on_chip(join_kernel, [shape((SIDE * (rows + own), own), bf16)], [packed, to_side(packed)])[0]
    blocks = gather_ring(joined)
    early = on_chip(
        functools.partial(square_kernel, rows),
        [shape((rows, own))],
        [blocks[k] for k in range(RING) if k != far],
    )[0]
    dt_wide = jnp.pad(dt_weight.T, ((0, 128 - heads), (0, 0)))
    small = jnp.zeros((8 + groups, own), f32)
    small = small.at[0, :heads].set(dt_bias).at[1, :heads].set(decay_rate).at[2, :heads].set(skip_gain)
    small = small.at[8:].set(norm_gain.reshape(groups, own))
    normed, bc_mine = on_chip(
        functools.partial(norm_kernel, rows),
        [shape((rows, model), bf16), shape((model, state_n), bf16)],
        [*blocks, early, small],
        place,
    )
    bc_other = to_core(bc_mine)
    x, tailed, cums, step = on_chip(
        functools.partial(project_kernel, heads, size_p),
        [shape((rows, width)), shape((rows, width)), shape((HEADS, rows)), shape((HEADS, rows))],
        [normed, x_weight, dt_wide, small],
        flops=2 * rows * model * (width + 128),
    )
    both, slots = on_chip(
        functools.partial(state_kernel, size_p),
        [shape((rows, 2 * state_n)), shape((ROW, state_n + 16, half), bf16)],
        [normed, tailed, bc_mine, bc_other, cums],
        place,
        flops=2 * rows * model * 2 * state_n,
    )
    lines = sections // ROW
    by_row = [list(range(r * ROW, (r + 1) * ROW)) for r in range(lines)]
    row_total, enter_own, enter_pair, logs = on_chip(
        row_kernel,
        [shape((state_n + 16, half), bf16), shape((state_n, half)), shape((state_n, half)), shape((8, half))],
        [lax.all_to_all(slots, "section", 0, 0, axis_index_groups=by_row)],
        place,
    )
    above = [to_row(row_total, k) for k in range(1, lines)]
    result, opened, done = on_chip(
        functools.partial(scan_kernel, heads, size_p, 256),
        [shape((rows, width)), shape((rows, width)), shape((8, 128))],
        [normed, gate_weight, x, both, cums, step, small, logs],
        flops=2 * rows * model * width + 12 * rows * 256 * (width + 3 * state_n),
        transcendentals=heads * rows * 256,
    )
    keep, send = on_chip(
        prefix_kernel,
        [shape((state_n, half), bf16), shape((state_n, half), bf16)],
        [enter_own, enter_pair, logs, done, *above],
    )
    rest = to_core(send)
    soon, later = (far, far - 1), tuple(k for k in range(RING) if k not in (far, far - 1))
    ynorm, *early = on_chip(
        functools.partial(finish_kernel, size_p, soon),
        [shape((rows, width), bf16)] + [shape((SIDE * rows, own), bf16)] * len(soon),
        [result, opened, both, cums, keep, rest, out_gain.reshape(1, width), out_weight],
        place,
        flops=2 * rows * width * (2 * SIDE * own + 4 * width),
    )
    late = on_chip(
        functools.partial(share_kernel, later),
        [shape((SIDE * rows, own), bf16)] * len(later),
        [ynorm, out_weight],
        place,
        flops=2 * rows * width * len(later) * SIDE * own,
    )
    made = dict(zip(soon + later, [*early, *late]))
    shares = [made[k] for k in range(RING)]
    summed = reduce_ring(shares)
    return tokens.astype(f32) + summed[:rows] + to_side(summed[rows:].astype(bf16)).astype(f32)


def solution(mesh):
    return jax.shard_map(
        local,
        mesh=mesh,
        in_specs=(
            P("section", "head"),
            P(),
            P(None, "head"),
            P(None, "head"),
            P(None, "head"),
            P("head"),
            P("head"),
            P("head"),
            P("head", None),
            P("head"),
            P("head", None),
        ),
        out_specs=P("section", "head"),
        check_vma=False,
    )
```
